256 devices in a mesh: section: 4 (over y), band: 16 (over z, core), rep: 4 (over x).
Axes of the slice: x: 4, y: 4, z: 8, core: 2. Of those that a mesh axis runs over, the one named last changes fastest.
Arguments:
- images: bfloat16 [8, 64, 64, 128], P('rep', None, 'band'), may hold values from -6 to 6
- weights: bfloat16 [4, 3, 3, 3, 64, 64], P('section'), may hold values from -0.25 to 0.25
- cotangent: bfloat16 [8, 64, 64, 128], P('rep', None, 'band'), may hold values from -6 to 6
Outputs:
- section_acts: bfloat16 [4, 8, 64, 64, 128], P('section', 'rep', None, 'band')
- input_grads: bfloat16 [4, 8, 64, 64, 128], P('section', 'rep', None, 'band')
- weight_grads: float32 [4, 3, 3, 3, 64, 64], P('section')
The draws below stay inside these ranges and needn't reach their ends.
All inputs are finite; a program needn't handle non-finite values.
Results may differ from the reference program's by a relative error of at most 0.029.
Values may be sent and summed in bfloat16 or wider, within the bound.
No kernel may reach another device: no remote copies, remote signals or barrier semaphores. Data moves between devices by JAX's collectives and lax.ppermute only.
A program may use at most 128 MiB of HBM per device.

```python
import jax
import jax.numpy as jnp
from jax import lax

C = 64
WID = 128
B = 8
H = 64
N_SECTION = 4


def levels(stream_key, dims, split, low, top_value):
    factor_of, own = 1.0, jax.random.fold_in(stream_key, 6)
    for dim, blocks in split:
        steps = jnp.exp(jax.random.uniform(jax.random.fold_in(own, dim), (blocks,), jnp.float32, low / len(split), top_value / len(split)))
        factor_of = factor_of * jnp.repeat(steps, dims[dim] // blocks).reshape([-1 if axis == dim else 1 for axis in range(len(dims))])
    return factor_of


def gaussian(stream_key, extent, scale, bound, shards=(), kind=jnp.bfloat16):
    result = jax.random.normal(stream_key, extent, jnp.float32) * scale
    if len(shards) > 0:
        result = levels(stream_key, extent, shards, -0.22, 0.18) * result
    return jnp.clip(result, min=-bound, max=bound).astype(kind)


def setup_inputs(seed: int = 0) -> dict:
    key_list = jax.random.split(jax.random.key(seed), 4)
    images = gaussian(key_list[0], (B, C, H, WID), 1.0, 6.0, ((0, 4), (2, 16)))
    weights = gaussian(key_list[1], (N_SECTION, 3, 3, 3, C, C), (9 * C) ** -0.5, 0.25, ((0, 4),))
    cotangent = gaussian(key_list[2], (B, C, H, WID), 1.0, 6.0, ((0, 4), (2, 16)))
    return dict(images=images, weights=weights, cotangent=cotangent)


gelu_scale = 0.7978845608028654
cubic_coef = 0.044715

def gelu_value(values):
    inner = gelu_scale * (values + cubic_coef * values * values * values)
    return 0.5 * values * (1.0 + jnp.tanh(inner))

def gelu_slope(values):
    square = values * values
    tangent = jnp.tanh(gelu_scale * (values + cubic_coef * square * values))
    return 0.5 * (1.0 + tangent) + 0.5 * values * (1.0 - tangent * tangent) * gelu_scale * (1.0 + 3.0 * cubic_coef * square)

def conv_rows(padded, kernel):
    return lax.conv_general_dilated(padded, kernel, (1, 1), ((0, 0), (1, 1)), dimension_numbers=('NCHW', 'HWIO', 'NCHW'), preferred_element_type=jnp.float32)

def flipped(kernel):
    return jnp.swapaxes(kernel[::-1, ::-1], 2, 3)

def kernel_grad(padded, grad_out):
    summed = lax.conv_general_dilated(padded, grad_out, (1, 1), ((0, 0), (1, 1)), dimension_numbers=('CNHW', 'IOHW', 'NCHW'), preferred_element_type=jnp.float32)
    return jnp.transpose(summed, (2, 3, 0, 1))

def pad_rows(field):
    return jnp.pad(field, ((0, 0), (0, 0), (1, 1), (0, 0)))

def reference(images, weights, cotangent):
    sections = weights.shape[0]
    current = images
    outputs = []
    kept = []
    for section in range(sections):
        kernels = weights[section]
        ext_input = pad_rows(current)
        pre_first = conv_rows(ext_input, kernels[0])
        ext_first = pad_rows(gelu_value(pre_first).astype(jnp.bfloat16))
        pre_second = conv_rows(ext_first, kernels[1])
        ext_second = pad_rows(gelu_value(pre_second).astype(jnp.bfloat16))
        current = (current.astype(jnp.float32) + conv_rows(ext_second, kernels[2])).astype(jnp.bfloat16)
        outputs.append(current)
        kept.append((ext_input, ext_first, ext_second, pre_first, pre_second))
    grad_out = cotangent
    input_grads = [None] * sections
    kernel_grads = [None] * sections
    for section in reversed(range(sections)):
        kernels = weights[section]
        ext_input, ext_first, ext_second, pre_first, pre_second = kept[section]
        grad_third = kernel_grad(ext_second, grad_out)
        grad_act_two = conv_rows(pad_rows(grad_out), flipped(kernels[2]))
        grad_pre_two = (grad_act_two * gelu_slope(pre_second)).astype(jnp.bfloat16)
        grad_second = kernel_grad(ext_first, grad_pre_two)
        grad_act_one = conv_rows(pad_rows(grad_pre_two), flipped(kernels[1]))
        grad_pre_one = (grad_act_one * gelu_slope(pre_first)).astype(jnp.bfloat16)
        grad_first = kernel_grad(ext_input, grad_pre_one)
        grad_out = (grad_out.astype(jnp.float32) + conv_rows(pad_rows(grad_pre_one), flipped(kernels[0]))).astype(jnp.bfloat16)
        input_grads[section] = grad_out
        kernel_grads[section] = jnp.stack([grad_first, grad_second, grad_third])
    return (jnp.stack(outputs), jnp.stack(input_grads), jnp.stack(kernel_grads))
```

```python
import jax
import jax.numpy as jnp
from jax import lax
from jax.experimental import pallas as pl
from jax.experimental.pallas import tpu as pltpu
from jax.sharding import PartitionSpec as P

BF = jnp.bfloat16
F32 = jnp.float32
gelu_scale = 0.7978845608028654
cubic_coef = 0.044715

C = 64
WID = 128
ROWS = 64
OWN = 8
OFF = 24
WINDOW = 56
DEPTH = 4


def weight_blocks_kernel(where_ref, w0, w1, w2, w3, fwd_ref, bwd_ref):
    zero = jnp.zeros((C, C), F32)
    for hop, piece in enumerate((w0, w1, w2, w3)):
        section = lax.rem(where_ref[0] - hop + DEPTH, DEPTH)

        def one_layer(layer, carry, piece=piece, section=section):
            slot = section * 3 + layer
            for kw in range(3):
                taps = []
                for kh in range(3):
                    at = pl.multiple_of(layer * 288 + (kh * 3 + kw) * 32, 32)
                    block = piece[pl.ds(at, 32), :].astype(F32)
                    taps.append(jnp.concatenate([block[:, :C], block[:, C:]], axis=0))
                low = jnp.concatenate([taps[0], taps[1]], axis=0).T
                high = jnp.concatenate([taps[2], zero], axis=0).T
                low_up = jnp.concatenate([zero, taps[0]], axis=0).T
                high_up = jnp.concatenate([taps[1], taps[2]], axis=0).T
                first = jnp.concatenate([low, high], axis=1)
                second = jnp.concatenate([low_up, high_up], axis=1)
                fwd_ref[slot, pl.ds(kw * 128, 128), :] = jnp.concatenate(
                    [first, second], axis=0
                ).astype(BF)
                first = jnp.concatenate([taps[2], taps[1], taps[0], zero], axis=1)
                second = jnp.concatenate([zero, taps[2], taps[1], taps[0]], axis=1)
                bwd_ref[slot, pl.ds((2 - kw) * 128, 128), :] = jnp.concatenate(
                    [first, second], axis=0
                ).astype(BF)
            return carry

        lax.fori_loop(0, 3, one_layer, 0)


def sections_kernel(
    where_ref,
    im_c, im_l1, im_r1, im_l2, im_r2, im_l3, im_r3,
    wf_ref, wb_ref,
    keep_ref, send_ref, wg_ref,
    h_ref, a1_ref, a2_ref, p1_ref, p2_ref, g_ref, gp1_ref, gp2_ref,
):
    mine = where_ref[0]
    first_row = where_ref[1]
    core = where_ref[2]
    h_ref[0, 24:32] = im_c[0:8]
    h_ref[0, 16:24] = im_l1[0:8]
    h_ref[0, 32:40] = im_r1[0:8]
    h_ref[0, 8:16] = im_l2[0:8]
    h_ref[0, 40:48] = im_r2[0:8]
    h_ref[0, 2:8] = im_l3[...]
    h_ref[0, 48:54] = im_r3[...]
    g_ref[24:32] = im_c[8:16]
    g_ref[16:24] = im_l1[8:16]
    g_ref[32:40] = im_r1[8:16]
    g_ref[12:16] = im_l2[8:12]
    g_ref[40:44] = im_r2[8:12]

    lane = lax.broadcasted_iota(jnp.int32, (128, WID), 1)
    not_first = lane > 0
    not_last = lane < WID - 1

    def inside(row):
        at = row - OFF + first_row
        return jnp.logical_and(at >= 0, at < ROWS)

    def conv_loop(reach, source, slab, finish):
        start = OFF - reach
        steps = 2 + (reach + 1) // 2

        def step(t, carry):
            row = start + 4 * t
            low = source[pl.ds(row - 1, 4)].reshape(4 * C, WID)
            high = source[pl.ds(row + 1, 4)].reshape(4 * C, WID)
            product = lax.dot_general(
                slab[...],
                jnp.concatenate([low, high], axis=1),
                (((1,), (0,)), ((), ())),
                preferred_element_type=F32,
            )
            for half in range(2):
                part = product[:, half * WID:(half + 1) * WID]
                total = (
                    part[128:256]
                    + jnp.where(not_first, pltpu.roll(part[0:128], 1, 1), 0.0)
                    + jnp.where(not_last, pltpu.roll(part[256:384], WID - 1, 1), 0.0)
                )
                for one in range(2):
                    finish(row + 2 * half + one, total[one * C:(one + 1) * C])
            return carry

        lax.fori_loop(0, steps, step, 0)

    def tangent_of(values):
        return jnp.tanh(values * (gelu_scale + (gelu_scale * cubic_coef) * (values * values)))

    def slope_of(values):
        square = values * values
        tangent = jnp.tanh(values * (gelu_scale + (gelu_scale * cubic_coef) * square))
        return 0.5 * (1.0 + tangent) + (0.5 * values) * (1.0 - tangent * tangent) * (
            gelu_scale + (3.0 * gelu_scale * cubic_coef) * square
        )

    def forward(section, carry):
        def activate(pre_ref, act_ref):
            def finish(row, values):
                pre_ref[section, row] = values
                half = 0.5 * values
                act = half + half * tangent_of(values)
                act_ref[section, row] = jnp.where(inside(row), act, 0.0).astype(BF)

            return finish

        def residual(row, values):
            result = h_ref[section, row].astype(F32) + values
            h_ref[section + 1, row] = jnp.where(inside(row), result, 0.0).astype(BF)

        slot = section * 3
        conv_loop(21 - 3 * section, h_ref.at[section], wf_ref.at[slot],
                  activate(p1_ref, a1_ref))
        conv_loop(20 - 3 * section, a1_ref.at[section], wf_ref.at[slot + 1],
                  activate(p2_ref, a2_ref))
        conv_loop(jnp.where(section == DEPTH - 1, 0, 19 - 3 * section), a2_ref.at[section],
                  wf_ref.at[slot + 2], residual)
        return carry

    lax.fori_loop(0, DEPTH, forward, 0)

    def kernel_grad(layer, source, grads):
        wide_in, wide_out = [], []
        for row in range(OFF, OFF + OWN):
            wide_in.append(source[pl.ds(row - 1, 3)].reshape(3 * C, WID))
            out = grads[row].astype(F32)
            after = jnp.where(not_last[:C], pltpu.roll(out, WID - 1, 1), 0.0)
            before = jnp.where(not_first[:C], pltpu.roll(out, 1, 1), 0.0)
            wide_out.append(jnp.concatenate([after, out, before], axis=0).astype(BF))
        result = lax.dot_general(
            jnp.concatenate(wide_in, axis=1),
            jnp.concatenate(wide_out, axis=1),
            (((1,), (1,)), ((), ())),
            preferred_element_type=F32,
        )
        for kw in range(3):
            part = result[:, kw * C:(kw + 1) * C]
            packed = jnp.concatenate([part[:96], part[96:]], axis=1)
            wg_ref[pl.ds((layer * 3 + kw) * 96, 96), :] = packed.astype(BF)

    wg_ref[864:1024, :] = jnp.zeros((160, 128), BF)

    def backward(turn, carry):
        section = DEPTH - 1 - turn
        slot = section * 3

        @pl.when(section == mine)
        def _():
            kernel_grad(2, a2_ref.at[section], g_ref)

        def through(pre_ref, target):
            def finish(row, values):
                result = values * slope_of(pre_ref[section, row])
                target[row] = jnp.where(inside(row), result, 0.0).astype(BF)

            return finish

        def residual(row, values):
            result = g_ref[row].astype(F32) + values
            g_ref[row] = jnp.where(inside(row), result, 0.0).astype(BF)

        conv_loop(2 + 3 * section, g_ref, wb_ref.at[slot + 2], through(p2_ref, gp2_ref))
        conv_loop(1 + 3 * section, gp2_ref, wb_ref.at[slot + 1], through(p1_ref, gp1_ref))

        @pl.when(section == mine)
        def _():
            kernel_grad(1, a1_ref.at[section], gp2_ref)
            kernel_grad(0, h_ref.at[section], gp1_ref)

        conv_loop(3 * section, gp1_ref, wb_ref.at[slot], residual)
        return carry

    lax.fori_loop(0, DEPTH - mine, backward, 0)

    kept = OFF + 4 * core
    sent = OFF + 4 * (1 - core)
    keep_ref[0] = h_ref[mine + 1, pl.ds(kept, 4)]
    keep_ref[1] = g_ref[pl.ds(kept, 4)]
    send_ref[0] = h_ref[mine + 1, pl.ds(sent, 4)]
    send_ref[1] = g_ref[pl.ds(sent, 4)]


def unpack_kernel(sum_ref, out_ref):
    for layer in range(3):
        for kw in range(3):
            base = (layer * 3 + kw) * 96
            block = sum_ref[base:base + 96, :].astype(F32)
            tall = jnp.concatenate([block[:, :C], block[:, C:]], axis=0)
            for kh in range(3):
                out_ref[0, layer, kh, kw] = tall[kh * C:(kh + 1) * C]


def vmem(count):
    return [pl.BlockSpec(memory_space=pltpu.VMEM)] * count


def on_device(images, weights, cotangent):
    section = lax.axis_index("section")
    band = lax.axis_index("band")
    core = band % 2
    where = jnp.stack([section, (band // 2) * OWN, core]).astype(jnp.int32)

    field = jnp.stack([images, cotangent]).transpose(1, 0, 3, 2, 4)
    mine = jnp.where(core == 0, field[0], field[1])
    other = jnp.where(core == 0, field[1], field[0])
    bands = lax.axis_size("band")
    swapped = [(i, i ^ 1) for i in range(bands)]
    got = lax.ppermute(other, "band", swapped)
    center = jnp.where(
        core == 0,
        jnp.concatenate([mine, got], axis=1),
        jnp.concatenate([got, mine], axis=1),
    ).reshape(16, C, WID)

    def chips_away(value, chips):
        pairs = [(i, i + 2 * chips) for i in range(bands) if 0 <= i + 2 * chips < bands]
        return lax.ppermute(value, "band", pairs)

    left1 = chips_away(center, 1)
    right1 = chips_away(center, -1)
    left2 = chips_away(jnp.concatenate([center[0:8], center[12:16]]), 2)
    right2 = chips_away(center[0:12], -2)
    left3 = chips_away(center[2:8], 3)
    right3 = chips_away(center[0:6], -3)

    raw = weights.reshape(27, 2, 32, C)
    raw = jnp.concatenate([raw[:, 0], raw[:, 1]], axis=-1).reshape(864, 128)
    around = [
        lax.ppermute(raw, "section", [(i, (i + hop) % DEPTH) for i in range(DEPTH)])
        for hop in range(1, DEPTH)
    ]
    fwd, bwd = pl.pallas_call(
        weight_blocks_kernel,
        out_shape=[jax.ShapeDtypeStruct((12, 384, 256), BF)] * 2,
        in_specs=[pl.BlockSpec(memory_space=pltpu.SMEM)] + vmem(4),
        out_specs=vmem(2),
        name="weight_blocks",
    )(where, raw, *around)

    window = (WINDOW, C, WID)
    keep, send, grads = pl.pallas_call(
        sections_kernel,
        out_shape=[
            jax.ShapeDtypeStruct((2, 4, C, WID), BF),
            jax.ShapeDtypeStruct((2, 4, C, WID), BF),
            jax.ShapeDtypeStruct((1024, 128), BF),
        ],
        in_specs=[pl.BlockSpec(memory_space=pltpu.SMEM)] + vmem(9),
        out_specs=vmem(3),
        scratch_shapes=[
            pltpu.VMEM((DEPTH + 1,) + window, BF),
            pltpu.VMEM((DEPTH,) + window, BF),
            pltpu.VMEM((DEPTH,) + window, BF),
            pltpu.VMEM((DEPTH,) + window, F32),
            pltpu.VMEM((DEPTH,) + window, F32),
            pltpu.VMEM(window, BF),
            pltpu.VMEM(window, BF),
            pltpu.VMEM(window, BF),
        ],
        compiler_params=pltpu.CompilerParams(vmem_limit_bytes=48 * 1024 * 1024),
        name="sections",
    )(where, center, left1, right1, left2, right2, left3, right3, fwd, bwd)

    received = lax.ppermute(send, "band", swapped)
    zero = jnp.where(core == 0, keep, received)
    one = jnp.where(core == 0, received, keep)
    both = jnp.stack([zero, one]).transpose(1, 0, 3, 2, 4)

    parts = lax.all_to_all(grads.reshape(64, 16, 128), ("rep", "band"), 0, 0, tiled=True)
    total = jnp.sum(parts.astype(F32), axis=0).astype(BF)
    summed = lax.all_to_all(
        jnp.broadcast_to(total[None], (64, 16, 128)), ("rep", "band"), 0, 0, tiled=True
    ).reshape(1024, 128)
    weight_grads = pl.pallas_call(
        unpack_kernel,
        out_shape=jax.ShapeDtypeStruct((1, 3, 3, 3, C, C), F32),
        in_specs=vmem(1),
        out_specs=pl.BlockSpec(memory_space=pltpu.VMEM),
        name="unpack",
    )(summed)
    return both[0][None], both[1][None], weight_grads


def solution(mesh):
    in_specs = (
        P("rep", None, "band", None),
        P("section", None, None, None, None, None),
        P("rep", None, "band", None),
    )
    out_specs = (
        P("section", "rep", None, "band", None),
        P("section", "rep", None, "band", None),
        P("section", None, None, None, None, None),
    )
    return jax.shard_map(
        on_device, mesh=mesh, in_specs=in_specs, out_specs=out_specs, check_vma=False
    )
```

```python
import jax
import jax.numpy as jnp
from jax import lax
from jax.experimental import pallas as pl
from jax.experimental.pallas import tpu as pltpu
from jax.sharding import PartitionSpec as P

BF = jnp.bfloat16
F32 = jnp.float32
gelu_scale = 0.7978845608028654
cubic_coef = 0.044715

C = 64
WID = 128
ROWS = 64
OWN = 8
OFF = 24
WINDOW = 56
DEPTH = 4


def weight_blocks_kernel(where_ref, own, near, half, other, fwd_ref, bwd_ref, far):
    zero = jnp.zeros((C, C), BF)
    same = (
        lax.broadcasted_iota(jnp.int32, (C, C), 0) == lax.broadcasted_iota(jnp.int32, (C, C), 1)
    ).astype(F32).astype(BF)
    core = where_ref[2]
    far[pl.ds(pl.multiple_of(416 * core, 32), 448), :] = half[...]
    far[pl.ds(pl.multiple_of(416 * (1 - core), 32), 448), :] = other[864:1312, :]
    for piece, hop in ((own, 0), (near, 1 + 2 * core), (other, 3 - 2 * core), (far, 2)):
        section = lax.rem(where_ref[0] - hop + DEPTH, DEPTH)
        for layer in range(3):
            slot = section * 3 + layer
            for kw in range(3):
                taps = []
                for kh in range(3):
                    at = layer * 288 + (kh * 3 + kw) * 32
                    block = piece[at:at + 32, :]
                    taps.append(jnp.concatenate([block[:, :C], block[:, C:]], axis=0))
                tall = jnp.concatenate(taps + [zero] + [zero] + taps, axis=0)
                flat = lax.dot_general(
                    same, tall, (((1,), (1,)), ((), ())), preferred_element_type=F32
                ).astype(BF)
                here = slice(kw * 256, kw * 256 + 256)
                fwd_ref[slot, 0:C, here] = flat[:, 0:256]
                fwd_ref[slot, C:2 * C, here] = flat[:, 256:512]
                there = (2 - kw) * 256
                left = jnp.concatenate([taps[2], taps[1]], axis=1)
                middle = jnp.concatenate([taps[1], taps[0]], axis=1)
                bwd_ref[slot, 0:C, there:there + 128] = left
                bwd_ref[slot, 0:C, there + 128:there + 256] = jnp.concatenate([taps[0], zero], axis=1)
                bwd_ref[slot, C:2 * C, there:there + 128] = jnp.concatenate([zero, taps[2]], axis=1)
                bwd_ref[slot, C:2 * C, there + 128:there + 256] = middle


def sections_kernel(
    where_ref,
    im_c, im_l1, im_r1, im_l2, im_r2, im_l3, im_r3,
    wf_ref, wb_ref,
    keep_ref, send_ref, wg_ref,
    h_ref, a1_ref, a2_ref, p1_ref, p2_ref, g_ref, gp1_ref, gp2_ref,
):
    mine = where_ref[0]
    first_row = where_ref[1]
    core = where_ref[2]
    h_ref[0, 24:32] = im_c[0:8]
    h_ref[0, 16:24] = im_l1[0:8]
    h_ref[0, 32:40] = im_r1[0:8]
    h_ref[0, 8:16] = im_l2[0:8]
    h_ref[0, 40:48] = im_r2[0:8]
    h_ref[0, 2:8] = im_l3[...]
    h_ref[0, 48:54] = im_r3[...]
    g_ref[DEPTH, 24:32] = im_c[8:16]
    g_ref[DEPTH, 16:24] = im_l1[8:16]
    g_ref[DEPTH, 32:40] = im_r1[8:16]
    g_ref[DEPTH, 12:16] = im_l2[8:12]
    g_ref[DEPTH, 40:44] = im_r2[8:12]

    lane = lax.broadcasted_iota(jnp.int32, (128, WID), 1)
    not_first = lane > 0
    not_last = lane < WID - 1
    lane1 = lax.broadcasted_iota(jnp.int32, (1, WID), 1)
    keep_first = (lane1 > 0).astype(F32).astype(BF)
    keep_last = (lane1 < WID - 1).astype(F32).astype(BF)

    def inside(row):
        at = row - OFF + first_row
        return jnp.logical_and(at >= 0, at < ROWS)

    def conv_rows(row, count, source, slab, finish):
        rows = source[pl.ds(row - 1, count + 2)].reshape((count + 2) * C, WID)
        before = pltpu.roll(rows, 1, 1) * keep_first
        after = pltpu.roll(rows, WID - 1, 1) * keep_last
        products = []
        for at in range(0, count, 4):
            halves = []
            for part in (at, at + 2):
                cut = slice(part * C, (part + 4) * C)
                halves.append(jnp.concatenate([before[cut], rows[cut], after[cut]], axis=0))
            products.append(lax.dot_general(
                slab[...],
                jnp.concatenate(halves, axis=1),
                (((1,), (0,)), ((), ())),
                preferred_element_type=F32,
            ))
        for at, product in zip(range(0, count, 4), products):
            for half in range(2):
                for one in range(2):
                    finish(row + at + 2 * half + one, product[one * C:(one + 1) * C, half * WID:(half + 1) * WID])

    def conv_loop(reach, source, slab, finish):
        start = OFF - reach
        count = -(-(8 + 2 * reach) // 4) * 4
        parts = -(-count // 28)
        size = -(-count // (4 * parts)) * 4
        for part in range(parts):
            @pl.when(mine >= 0)
            def _(part=part):
                conv_rows(start + size * part, min(size, count - size * part), source, slab, finish)

    def tangent_of(values):
        return jnp.tanh(values * (gelu_scale + (gelu_scale * cubic_coef) * (values * values)))

    def slope_of(values):
        square = values * values
        tangent = jnp.tanh(values * (gelu_scale + (gelu_scale * cubic_coef) * square))
        return 0.5 * (1.0 + tangent) + (0.5 * values) * (1.0 - tangent * tangent) * (
            gelu_scale + (3.0 * gelu_scale * cubic_coef) * square
        )

    def forward(section, carry):
        def activate(pre_ref, act_ref):
            def finish(row, values):
                pre_ref[section, row] = values
                half = 0.5 * values
                act = half + half * tangent_of(values)
                act_ref[section, row] = jnp.where(inside(row), act, 0.0).astype(BF)

            return finish

        def residual(row, values):
            result = h_ref[section, row].astype(F32) + values
            h_ref[section + 1, row] = jnp.where(inside(row), result, 0.0).astype(BF)

        slot = section * 3
        conv_loop(21 - 3 * section, h_ref.at[section], wf_ref.at[slot],
                  activate(p1_ref, a1_ref))
        conv_loop(20 - 3 * section, a1_ref.at[section], wf_ref.at[slot + 1],
                  activate(p2_ref, a2_ref))
        conv_loop(0 if section == DEPTH - 1 else 19 - 3 * section, a2_ref.at[section],
                  wf_ref.at[slot + 2], residual)
        return carry

    for section in range(DEPTH):
        forward(section, 0)

    def kernel_grad(layer, source, grads):
        wide_in, wide_out = [], []
        for row in range(OFF, OFF + OWN):
            wide_in.append(source[pl.ds(row - 1, 3)].reshape(3 * C, WID))
            out = grads[row].astype(F32)
            after = jnp.where(not_last[:C], pltpu.roll(out, WID - 1, 1), 0.0)
            before = jnp.where(not_first[:C], pltpu.roll(out, 1, 1), 0.0)
            wide_out.append(jnp.concatenate([after, out, before], axis=0).astype(BF))
        result = lax.dot_general(
            jnp.concatenate(wide_in, axis=1),
            jnp.concatenate(wide_out, axis=1),
            (((1,), (1,)), ((), ())),
            preferred_element_type=F32,
        )
        for kw in range(3):
            part = result[:, kw * C:(kw + 1) * C]
            packed = jnp.concatenate([part[:96], part[96:]], axis=1)
            wg_ref[pl.ds((layer * 3 + kw) * 96, 96), :] = packed.astype(BF)

    wg_ref[864:1024, :] = jnp.zeros((160, 128), BF)

    def backward(turn, carry):
        section = DEPTH - 1 - turn
        slot = section * 3

        def through(pre_ref, target):
            def finish(row, values):
                result = values * slope_of(pre_ref[section, row])
                target[section, row] = jnp.where(inside(row), result, 0.0).astype(BF)

            return finish

        def residual(row, values):
            result = g_ref[section + 1, row].astype(F32) + values
            g_ref[section, row] = jnp.where(inside(row), result, 0.0).astype(BF)

        conv_loop(2 + 3 * section, g_ref.at[section + 1], wb_ref.at[slot + 2], through(p2_ref, gp2_ref))
        conv_loop(1 + 3 * section, gp2_ref.at[section], wb_ref.at[slot + 1], through(p1_ref, gp1_ref))

        conv_loop(3 * section, gp1_ref.at[section], wb_ref.at[slot], residual)
        return carry

    for turn in range(DEPTH):
        backward(turn, 0)

    kernel_grad(2, a2_ref.at[mine], g_ref.at[mine + 1])
    kernel_grad(1, a1_ref.at[mine], gp2_ref.at[mine])
    kernel_grad(0, h_ref.at[mine], gp1_ref.at[mine])

    kept = OFF + 4 * core
    sent = OFF + 4 * (1 - core)
    keep_ref[0] = h_ref[mine + 1, pl.ds(kept, 4)]
    keep_ref[1] = g_ref[mine, pl.ds(kept, 4)]
    send_ref[0] = h_ref[mine + 1, pl.ds(sent, 4)]
    send_ref[1] = g_ref[mine, pl.ds(sent, 4)]


def unpack_kernel(sum_ref, out_ref):
    for layer in range(3):
        for kw in range(3):
            base = (layer * 3 + kw) * 96
            block = sum_ref[base:base + 96, :].astype(F32)
            tall = jnp.concatenate([block[:, :C], block[:, C:]], axis=0)
            for kh in range(3):
                out_ref[0, layer, kh, kw] = tall[kh * C:(kh + 1) * C]


def vmem(count):
    return [pl.BlockSpec(memory_space=pltpu.VMEM)] * count


def sections_call(where, pieces, fwd, bwd):
    window = (WINDOW, C, WID)
    return pl.pallas_call(
        sections_kernel,
        out_shape=[
            jax.ShapeDtypeStruct((2, 4, C, WID), BF),
            jax.ShapeDtypeStruct((2, 4, C, WID), BF),
            jax.ShapeDtypeStruct((1024, 128), BF),
        ],
        in_specs=[pl.BlockSpec(memory_space=pltpu.SMEM)] + vmem(9),
        out_specs=vmem(3),
        scratch_shapes=[
            pltpu.VMEM((DEPTH + 1,) + window, BF),
            pltpu.VMEM((DEPTH,) + window, BF),
            pltpu.VMEM((DEPTH,) + window, BF),
            pltpu.VMEM((DEPTH,) + window, F32),
            pltpu.VMEM((DEPTH,) + window, F32),
            pltpu.VMEM((DEPTH + 1,) + window, BF),
            pltpu.VMEM((DEPTH,) + window, BF),
            pltpu.VMEM((DEPTH,) + window, BF),
        ],
        compiler_params=pltpu.CompilerParams(vmem_limit_bytes=62 * 1024 * 1024),
        name="sections",
    )(where, *pieces, fwd, bwd)


def on_device(images, weights, cotangent):
    section = lax.axis_index("section")
    band = lax.axis_index("band")
    core = band % 2
    where = jnp.stack([section, (band // 2) * OWN, core]).astype(jnp.int32)

    field = jnp.stack([images, cotangent]).transpose(1, 0, 3, 2, 4)
    mine = jnp.where(core == 0, field[0], field[1])
    other = jnp.where(core == 0, field[1], field[0])
    bands = lax.axis_size("band")
    swapped = [(i, i ^ 1) for i in range(bands)]
    got = lax.ppermute(other, "band", swapped)
    center = jnp.where(
        core == 0,
        jnp.concatenate([mine, got], axis=1),
        jnp.concatenate([got, mine], axis=1),
    ).reshape(16, C, WID)

    def chips_away(value, chips):
        pairs = [(i, i + 2 * chips) for i in range(bands) if 0 <= i + 2 * chips < bands]
        return lax.ppermute(value, "band", pairs)

    left1 = chips_away(center, 1)
    right1 = chips_away(center, -1)
    left2 = chips_away(jnp.concatenate([center[0:8], center[12:16]]), 2)
    right2 = chips_away(center[0:12], -2)
    left3 = chips_away(center[2:8], 3)
    right3 = chips_away(center[0:6], -3)

    raw = weights.reshape(27, 2, 32, C)
    raw = jnp.concatenate([raw[:, 0], raw[:, 1]], axis=-1).reshape(864, 128)
    near = lax.ppermute(
        raw,
        ("section", "band"),
        [
            (s * bands + b, (s + 1 - 2 * (b % 2)) % DEPTH * bands + b)
            for s in range(DEPTH)
            for b in range(bands)
        ],
    )
    half = lax.ppermute(
        jnp.where(core == 0, raw[:448], raw[416:]),
        "section",
        [(s, (s + 2) % DEPTH) for s in range(DEPTH)],
    )
    other_weights = lax.ppermute(jnp.concatenate([near, half]), "band", swapped)
    fwd, bwd = pl.pallas_call(
        weight_blocks_kernel,
        out_shape=[jax.ShapeDtypeStruct((12, 128, 768), BF)] * 2,
        in_specs=[pl.BlockSpec(memory_space=pltpu.SMEM)] + vmem(4),
        out_specs=vmem(2),
        scratch_shapes=[pltpu.VMEM((864, 128), BF)],
        name="weight_blocks",
    )(where, raw, near, half, other_weights)

    keep, send, grads = sections_call(
        where, (center, left1, right1, left2, right2, left3, right3), fwd, bwd
    )

    received = lax.ppermute(send, "band", swapped)
    zero = jnp.where(core == 0, keep, received)
    one = jnp.where(core == 0, received, keep)
    both = jnp.stack([zero, one]).transpose(1, 0, 3, 2, 4)

    parts = lax.all_to_all(grads.reshape(64, 16, 128), ("rep", "band"), 0, 0, tiled=True)
    total = jnp.sum(parts.astype(F32), axis=0).astype(BF)
    summed = lax.all_to_all(
        jnp.broadcast_to(total[None], (64, 16, 128)), ("rep", "band"), 0, 0, tiled=True
    ).reshape(1024, 128)
    weight_grads = pl.pallas_call(
        unpack_kernel,
        out_shape=jax.ShapeDtypeStruct((1, 3, 3, 3, C, C), F32),
        in_specs=vmem(1),
        out_specs=pl.BlockSpec(memory_space=pltpu.VMEM),
        name="unpack",
    )(summed)
    return both[0][None], both[1][None], weight_grads


def solution(mesh):
    in_specs = (
        P("rep", None, "band", None),
        P("section", None, None, None, None, None),
        P("rep", None, "band", None),
    )
    out_specs = (
        P("section", "rep", None, "band", None),
        P("section", "rep", None, "band", None),
        P("section", None, None, None, None, None),
    )
    return jax.shard_map(
        on_device, mesh=mesh, in_specs=in_specs, out_specs=out_specs, check_vma=False
    )
```

```python
import jax
import jax.numpy as jnp
from jax import lax
from jax.experimental import pallas as pl
from jax.experimental.pallas import tpu as pltpu
from jax.sharding import PartitionSpec as P

BF = jnp.bfloat16
F32 = jnp.float32
gelu_scale = 0.7978845608028654
cubic_coef = 0.044715

C = 64
WID = 128
ROWS = 64
OWN = 8
OFF = 24
WINDOW = 56
DEPTH = 4
LOW = 19
KEPT = 20


def weight_blocks_kernel(where_ref, own, near, half, other, fwd_ref, bwd_ref, far):
    zero = jnp.zeros((C, C), BF)
    same = (
        lax.broadcasted_iota(jnp.int32, (C, C), 0) == lax.broadcasted_iota(jnp.int32, (C, C), 1)
    ).astype(F32).astype(BF)
    core = where_ref[2]
    far[pl.ds(pl.multiple_of(416 * core, 32), 448), :] = half[...]
    far[pl.ds(pl.multiple_of(416 * (1 - core), 32), 448), :] = other[864:1312, :]
    for piece, hop in ((own, 0), (near, 1 + 2 * core), (other, 3 - 2 * core), (far, 2)):
        section = lax.rem(where_ref[0] - hop + DEPTH, DEPTH)
        for layer in range(3):
            slot = section * 3 + layer
            for kw in range(3):
                taps = []
                for kh in range(3):
                    at = layer * 288 + (kh * 3 + kw) * 32
                    block = piece[at:at + 32, :]
                    taps.append(jnp.concatenate([block[:, :C], block[:, C:]], axis=0))
                tall = jnp.concatenate(taps + [zero] + [zero] + taps, axis=0)
                flat = lax.dot_general(
                    same, tall, (((1,), (1,)), ((), ())), preferred_element_type=F32
                ).astype(BF)
                here = slice(kw * 256, kw * 256 + 256)
                fwd_ref[slot, 0:C, here] = flat[:, 0:256]
                fwd_ref[slot, C:2 * C, here] = flat[:, 256:512]
                there = (2 - kw) * 256
                left = jnp.concatenate([taps[2], taps[1]], axis=1)
                middle = jnp.concatenate([taps[1], taps[0]], axis=1)
                bwd_ref[slot, 0:C, there:there + 128] = left
                bwd_ref[slot, 0:C, there + 128:there + 256] = jnp.concatenate([taps[0], zero], axis=1)
                bwd_ref[slot, C:2 * C, there:there + 128] = jnp.concatenate([zero, taps[2]], axis=1)
                bwd_ref[slot, C:2 * C, there + 128:there + 256] = middle


def conv_tools(where_ref):
    first_row = where_ref[1]
    lane = lax.broadcasted_iota(jnp.int32, (1, WID), 1)
    keep_first = (lane > 0).astype(F32).astype(BF)
    keep_last = (lane < WID - 1).astype(F32).astype(BF)

    def inside(row):
        at = row - OFF + first_row
        return jnp.logical_and(at >= 0, at < ROWS)

    def conv_rows(row, count, source, slab, finish):
        rows = source[pl.ds(row - 1, count + 2)].reshape((count + 2) * C, WID)
        before = pltpu.roll(rows, 1, 1) * keep_first
        after = pltpu.roll(rows, WID - 1, 1) * keep_last
        products = []
        for at in range(0, count, 4):
            halves = []
            for part in (at, at + 2):
                cut = slice(part * C, (part + 4) * C)
                halves.append(jnp.concatenate([before[cut], rows[cut], after[cut]], axis=0))
            products.append(
                lax.dot_general(
                    slab[...],
                    jnp.concatenate(halves, axis=1),
                    (((1,), (0,)), ((), ())),
                    preferred_element_type=F32,
                )
            )
        for at, product in zip(range(0, count, 4), products):
            for half in range(2):
                for one in range(2):
                    finish(
                        row + at + 2 * half + one,
                        product[one * C:(one + 1) * C, half * WID:(half + 1) * WID],
                    )

    def conv(reach, source, slab, finish):
        start = OFF - reach
        count = -(-(OWN + 2 * reach) // 4) * 4
        parts = -(-count // 28)
        size = -(-count // (4 * parts)) * 4
        for part in range(parts):

            @pl.when(where_ref[0] >= 0)
            def _(part=part):
                conv_rows(start + size * part, min(size, count - size * part), source, slab, finish)

    return inside, conv


def tangent_of(values):
    return jnp.tanh(values * (gelu_scale + (gelu_scale * cubic_coef) * (values * values)))


def slope_of(values):
    square = values * values
    tangent = jnp.tanh(values * (gelu_scale + (gelu_scale * cubic_coef) * square))
    return 0.5 * (1.0 + tangent) + (0.5 * values) * (1.0 - tangent * tangent) * (
        gelu_scale + (3.0 * gelu_scale * cubic_coef) * square
    )


def kernel_grad(layer, source, grads, wg_ref):
    lane = lax.broadcasted_iota(jnp.int32, (C, WID), 1)
    wide_in, wide_out = [], []
    for row in range(OWN):
        wide_in.append(source[pl.ds(row, 3)].reshape(3 * C, WID))
        out = grads[OFF + row].astype(F32)
        after = jnp.where(lane < WID - 1, pltpu.roll(out, WID - 1, 1), 0.0)
        before = jnp.where(lane > 0, pltpu.roll(out, 1, 1), 0.0)
        wide_out.append(jnp.concatenate([after, out, before], axis=0).astype(BF))
    result = lax.dot_general(
        jnp.concatenate(wide_in, axis=1),
        jnp.concatenate(wide_out, axis=1),
        (((1,), (1,)), ((), ())),
        preferred_element_type=F32,
    )
    for kw in range(3):
        part = result[:, kw * C:(kw + 1) * C]
        packed = jnp.concatenate([part[:96], part[96:]], axis=1)
        wg_ref[pl.ds((layer * 3 + kw) * 96, 96), :] = packed.astype(BF)


def back_section(where_ref, section, level, slot, reach, pre, grads, gp1_ref, gp2_ref, wb_ref):
    inside, conv = conv_tools(where_ref)

    def through(layer, target):
        def finish(row, values):
            result = values * slope_of(pre(section, layer, row))
            target[level, row] = jnp.where(inside(row), result, 0.0).astype(BF)

        return finish

    def residual(row, values):
        result = grads[level + 1, row].astype(F32) + values
        grads[level, row] = jnp.where(inside(row), result, 0.0).astype(BF)

    conv(reach + 2, grads.at[level + 1], wb_ref.at[slot + 2], through(1, gp2_ref))
    conv(reach + 1, gp2_ref.at[level], wb_ref.at[slot + 1], through(0, gp1_ref))
    conv(reach, gp1_ref.at[level], wb_ref.at[slot], residual)


def first_kernel(
    where_ref,
    im_c, im_l1, im_r1, im_l2, im_r2,
    wf_ref, wb_ref,
    act_keep_ref, act_send_ref, top_ref, edge_ref, pre_ref, in_ref, wg_ref,
    h_ref, a1_ref, a2_ref, p1_ref, p2_ref, g_ref, gp1_ref, gp2_ref,
):
    mine = where_ref[0]
    core = where_ref[2]
    inside, conv = conv_tools(where_ref)
    h_ref[0, 24:32] = im_c[0:8]
    h_ref[0, 16:24] = im_l1[0:8]
    h_ref[0, 32:40] = im_r1[0:8]
    h_ref[0, 8:16] = im_l2[...]
    h_ref[0, 40:48] = im_r2[...]
    g_ref[2, 24:32] = im_c[8:16]
    g_ref[2, 18:24] = im_l1[8:14]
    g_ref[2, 32:38] = im_r1[8:14]

    def activate(section, keep_ref, act_ref):
        def finish(row, values):
            keep_ref[section, row] = values
            half = 0.5 * values
            act = half + half * tangent_of(values)
            act_ref[section, row] = jnp.where(inside(row), act, 0.0).astype(BF)

        return finish

    for section in range(DEPTH):
        slot = section * 3

        def residual(row, values, section=section):
            result = h_ref[section, row].astype(F32) + values
            h_ref[section + 1, row] = jnp.where(inside(row), result, 0.0).astype(BF)

        conv(15 - 3 * section, h_ref.at[section], wf_ref.at[slot], activate(section, p1_ref, a1_ref))
        conv(14 - 3 * section, a1_ref.at[section], wf_ref.at[slot + 1], activate(section, p2_ref, a2_ref))
        conv(
            0 if section == DEPTH - 1 else 13 - 3 * section,
            a2_ref.at[section], wf_ref.at[slot + 2], residual,
        )

    def pre(section, layer, row):
        return (p2_ref if layer else p1_ref)[section, row]

    back_section(where_ref, 3, 1, 9, 3, pre, g_ref, gp1_ref, gp2_ref, wb_ref)
    back_section(where_ref, 2, 0, 6, 0, pre, g_ref, gp1_ref, gp2_ref, wb_ref)

    act_keep_ref[...] = h_ref[mine + 1, pl.ds(OFF + 4 * core, 4)]
    act_send_ref[...] = h_ref[mine + 1, pl.ds(OFF + 4 * (1 - core), 4)]
    edge_ref[...] = g_ref[0, OFF:OFF + OWN]
    for section in range(2):
        pre_ref[section, 0] = p1_ref[section, LOW:LOW + KEPT]
        pre_ref[section, 1] = p2_ref[section, LOW:LOW + KEPT]

    @pl.when(mine >= 2)
    def _():
        top_ref[...] = g_ref[mine - 2, OFF:OFF + OWN]
        kernel_grad(2, a2_ref.at[mine, OFF - 1:OFF + 9], g_ref.at[mine - 1], wg_ref)
        kernel_grad(1, a1_ref.at[mine, OFF - 1:OFF + 9], gp2_ref.at[mine - 2], wg_ref)
        kernel_grad(0, h_ref.at[mine, OFF - 1:OFF + 9], gp1_ref.at[mine - 2], wg_ref)
        wg_ref[864:1024, :] = jnp.zeros((160, 128), BF)
        in_ref[...] = jnp.zeros(in_ref.shape, BF)

    @pl.when(mine < 2)
    def _():
        top_ref[...] = jnp.zeros(top_ref.shape, BF)
        wg_ref[...] = jnp.zeros(wg_ref.shape, BF)
        in_ref[0] = h_ref[mine, OFF - 1:OFF + 9]
        in_ref[1] = a1_ref[mine, OFF - 1:OFF + 9]
        in_ref[2] = a2_ref[mine, OFF - 1:OFF + 9]


def second_kernel(
    where_ref,
    edge_ref, left_ref, right_ref, pre_ref, in_ref, top_ref, top_wg_ref, wb_ref,
    keep_ref, send_ref, wg_ref,
    g_ref, gp1_ref, gp2_ref,
):
    mine = where_ref[0]
    core = where_ref[2]
    g_ref[2, OFF:OFF + OWN] = edge_ref[...]
    g_ref[2, OFF - 6:OFF] = left_ref[...]
    g_ref[2, OFF + OWN:OFF + OWN + 6] = right_ref[...]

    @pl.when(mine < 2)
    def _():
        def pre(section, layer, row):
            return pre_ref[section, layer, row - LOW]

        back_section(where_ref, 1, 1, 3, 3, pre, g_ref, gp1_ref, gp2_ref, wb_ref)
        back_section(where_ref, 0, 0, 0, 0, pre, g_ref, gp1_ref, gp2_ref, wb_ref)
        kernel_grad(2, in_ref.at[2], g_ref.at[mine + 1], wg_ref)
        kernel_grad(1, in_ref.at[1], gp2_ref.at[mine], wg_ref)
        kernel_grad(0, in_ref.at[0], gp1_ref.at[mine], wg_ref)
        wg_ref[864:1024, :] = jnp.zeros((160, 128), BF)
        keep_ref[...] = g_ref[mine, pl.ds(OFF + 4 * core, 4)]
        send_ref[...] = g_ref[mine, pl.ds(OFF + 4 * (1 - core), 4)]

    @pl.when(mine >= 2)
    def _():
        wg_ref[...] = top_wg_ref[...]
        keep_ref[...] = top_ref[pl.ds(4 * core, 4)]
        send_ref[...] = top_ref[pl.ds(4 * (1 - core), 4)]


def unpack_kernel(sum_ref, out_ref):
    for layer in range(3):
        for kw in range(3):
            base = (layer * 3 + kw) * 96
            block = sum_ref[base:base + 96, :].astype(F32)
            tall = jnp.concatenate([block[:, :C], block[:, C:]], axis=0)
            for kh in range(3):
                out_ref[0, layer, kh, kw] = tall[kh * C:(kh + 1) * C]


def vmem(count):
    return [pl.BlockSpec(memory_space=pltpu.VMEM)] * count


WINDOW_SHAPE = (WINDOW, C, WID)


def first_call(where, pieces, fwd, bwd):
    return pl.pallas_call(
        first_kernel,
        out_shape=[
            jax.ShapeDtypeStruct((4, C, WID), BF),
            jax.ShapeDtypeStruct((4, C, WID), BF),
            jax.ShapeDtypeStruct((OWN, C, WID), BF),
            jax.ShapeDtypeStruct((OWN, C, WID), BF),
            jax.ShapeDtypeStruct((2, 2, KEPT, C, WID), F32),
            jax.ShapeDtypeStruct((3, 10, C, WID), BF),
            jax.ShapeDtypeStruct((1024, 128), BF),
        ],
        in_specs=[pl.BlockSpec(memory_space=pltpu.SMEM)] + vmem(7),
        out_specs=vmem(7),
        scratch_shapes=[
            pltpu.VMEM((DEPTH + 1,) + WINDOW_SHAPE, BF),
            pltpu.VMEM((DEPTH,) + WINDOW_SHAPE, BF),
            pltpu.VMEM((DEPTH,) + WINDOW_SHAPE, BF),
            pltpu.VMEM((DEPTH,) + WINDOW_SHAPE, F32),
            pltpu.VMEM((DEPTH,) + WINDOW_SHAPE, F32),
            pltpu.VMEM((3,) + WINDOW_SHAPE, BF),
            pltpu.VMEM((2,) + WINDOW_SHAPE, BF),
            pltpu.VMEM((2,) + WINDOW_SHAPE, BF),
        ],
        compiler_params=pltpu.CompilerParams(vmem_limit_bytes=58 * 1024 * 1024),
        name="first_part",
    )(where, *pieces, fwd, bwd)


def second_call(where, *arrays):
    return pl.pallas_call(
        second_kernel,
        out_shape=[
            jax.ShapeDtypeStruct((4, C, WID), BF),
            jax.ShapeDtypeStruct((4, C, WID), BF),
            jax.ShapeDtypeStruct((1024, 128), BF),
        ],
        in_specs=[pl.BlockSpec(memory_space=pltpu.SMEM)] + vmem(8),
        out_specs=vmem(3),
        scratch_shapes=[
            pltpu.VMEM((3,) + WINDOW_SHAPE, BF),
            pltpu.VMEM((2,) + WINDOW_SHAPE, BF),
            pltpu.VMEM((2,) + WINDOW_SHAPE, BF),
        ],
        compiler_params=pltpu.CompilerParams(vmem_limit_bytes=32 * 1024 * 1024),
        name="second_part",
    )(where, *arrays)


def on_device(images, weights, cotangent):
    section = lax.axis_index("section")
    band = lax.axis_index("band")
    core = band % 2
    where = jnp.stack([section, (band // 2) * OWN, core]).astype(jnp.int32)

    field = jnp.stack([images, cotangent]).transpose(1, 0, 3, 2, 4)
    mine = jnp.where(core == 0, field[0], field[1])
    other = jnp.where(core == 0, field[1], field[0])
    bands = lax.axis_size("band")
    swapped = [(i, i ^ 1) for i in range(bands)]
    got = lax.ppermute(other, "band", swapped)
    center = jnp.where(
        core == 0,
        jnp.concatenate([mine, got], axis=1),
        jnp.concatenate([got, mine], axis=1),
    ).reshape(16, C, WID)

    def chips_away(value, chips):
        pairs = [(i, i + 2 * chips) for i in range(bands) if 0 <= i + 2 * chips < bands]
        return lax.ppermute(value, "band", pairs)

    left1 = chips_away(jnp.concatenate([center[0:8], center[10:16]]), 1)
    right1 = chips_away(center[0:14], -1)
    left2 = chips_away(center[0:8], 2)
    right2 = chips_away(center[0:8], -2)

    raw = weights.reshape(27, 2, 32, C)
    raw = jnp.concatenate([raw[:, 0], raw[:, 1]], axis=-1).reshape(864, 128)
    near = lax.ppermute(
        raw,
        ("section", "band"),
        [
            (s * bands + b, (s + 1 - 2 * (b % 2)) % DEPTH * bands + b)
            for s in range(DEPTH)
            for b in range(bands)
        ],
    )
    half = lax.ppermute(
        jnp.where(core == 0, raw[:448], raw[416:]),
        "section",
        [(s, (s + 2) % DEPTH) for s in range(DEPTH)],
    )
    other_weights = lax.ppermute(jnp.concatenate([near, half]), "band", swapped)
    fwd, bwd = pl.pallas_call(
        weight_blocks_kernel,
        out_shape=[jax.ShapeDtypeStruct((12, 128, 768), BF)] * 2,
        in_specs=[pl.BlockSpec(memory_space=pltpu.SMEM)] + vmem(4),
        out_specs=vmem(2),
        scratch_shapes=[pltpu.VMEM((864, 128), BF)],
        name="weight_blocks",
    )(where, raw, near, half, other_weights)

    act_keep, act_send, top, edge, pre, inputs, top_wg = first_call(
        where, (center, left1, right1, left2, right2), fwd, bwd
    )
    edge_left = chips_away(edge[2:8], 1)
    edge_right = chips_away(edge[0:6], -1)
    act_got = lax.ppermute(act_send, "band", swapped)
    keep, send, grads = second_call(
        where, edge, edge_left, edge_right, pre, inputs, top, top_wg, bwd
    )
    got_back = lax.ppermute(send, "band", swapped)

    def placed(kept, received):
        zero = jnp.where(core == 0, kept, received)
        one = jnp.where(core == 0, received, kept)
        return jnp.stack([zero, one]).transpose(0, 2, 1, 3)[None]

    parts = lax.all_to_all(grads.reshape(64, 16, 128), ("rep", "band"), 0, 0, tiled=True)
    total = jnp.sum(parts.astype(F32), axis=0).astype(BF)
    summed = lax.all_to_all(
        jnp.broadcast_to(total[None], (64, 16, 128)), ("rep", "band"), 0, 0, tiled=True
    ).reshape(1024, 128)
    weight_grads = pl.pallas_call(
        unpack_kernel,
        out_shape=jax.ShapeDtypeStruct((1, 3, 3, 3, C, C), F32),
        in_specs=vmem(1),
        out_specs=pl.BlockSpec(memory_space=pltpu.VMEM),
        name="unpack",
    )(summed)
    return placed(act_keep, act_got), placed(keep, got_back), weight_grads


def solution(mesh):
    in_specs = (
        P("rep", None, "band", None),
        P("section", None, None, None, None, None),
        P("rep", None, "band", None),
    )
    out_specs = (
        P("section", "rep", None, "band", None),
        P("section", "rep", None, "band", None),
        P("section", None, None, None, None, None),
    )
    return jax.shard_map(
        on_device, mesh=mesh, in_specs=in_specs, out_specs=out_specs, check_vma=False
    )
```

```python
import jax
import jax.numpy as jnp
from jax import lax
from jax.experimental import pallas as pl
from jax.experimental.pallas import tpu as pltpu
from jax.sharding import Mesh
from jax.sharding import PartitionSpec as P

BF = jnp.bfloat16
F32 = jnp.float32
gelu_scale = 0.7978845608028654
cubic_coef = 0.044715

C = 64
WID = 128
ROWS = 64
OWN = 8
OFF = 24
WINDOW = 56
DEPTH = 4


def weight_blocks_kernel(where_ref, own, near, half, other, fwd_ref, bwd_ref, far):
    zero = jnp.zeros((C, C), BF)
    same = (
        lax.broadcasted_iota(jnp.int32, (C, C), 0) == lax.broadcasted_iota(jnp.int32, (C, C), 1)
    ).astype(F32).astype(BF)
    core = where_ref[2]
    far[pl.ds(pl.multiple_of(416 * core, 32), 448), :] = half[...]
    far[pl.ds(pl.multiple_of(416 * (1 - core), 32), 448), :] = other[864:1312, :]
    for piece, hop in ((own, 0), (near, 1 + 2 * core), (other, 3 - 2 * core), (far, 2)):
        section = lax.rem(where_ref[4] - hop + DEPTH, DEPTH)
        for layer in range(3):
            slot = section * 3 + layer
            for kw in range(3):
                taps = []
                for kh in range(3):
                    at = layer * 288 + (kh * 3 + kw) * 32
                    block = piece[at:at + 32, :]
                    taps.append(jnp.concatenate([block[:, :C], block[:, C:]], axis=0))
                tall = jnp.concatenate(taps + [zero] + [zero] + taps, axis=0)
                flat = lax.dot_general(
                    same, tall, (((1,), (1,)), ((), ())), preferred_element_type=F32
                ).astype(BF)
                here = slice(kw * 256, kw * 256 + 256)
                fwd_ref[slot, 0:C, here] = flat[:, 0:256]
                fwd_ref[slot, C:2 * C, here] = flat[:, 256:512]
                there = (2 - kw) * 256
                left = jnp.concatenate([taps[2], taps[1]], axis=1)
                middle = jnp.concatenate([taps[1], taps[0]], axis=1)
                bwd_ref[slot, 0:C, there:there + 128] = left
                bwd_ref[slot, 0:C, there + 128:there + 256] = jnp.concatenate([taps[0], zero], axis=1)
                bwd_ref[slot, C:2 * C, there:there + 128] = jnp.concatenate([zero, taps[2]], axis=1)
                bwd_ref[slot, C:2 * C, there + 128:there + 256] = middle


def sections_kernel(
    where_ref,
    mine_c, mine_l1, mine_r1, mine_l2, mine_r2, mine_l3, mine_r3, other_c, other_1, other_23,
    wf_ref, wb_ref,
    even_ref, odd_ref, wg_ref,
    h_ref, a1_ref, a2_ref, p1_ref, p2_ref, g_ref, gp1_ref, gp2_ref,
):
    mine = where_ref[0]
    first_row = where_ref[1]
    core = where_ref[2]
    here, there = 4 * core, 4 * (1 - core)
    mine_pieces = (mine_c, mine_l1, mine_r1, mine_l2, mine_r2, mine_l3, mine_r3)
    for piece, base in zip(mine_pieces, (24, 16, 32, 8, 40, 0, 48)):
        h_ref[0, pl.ds(base + here, 4)] = piece[0:4]
        if 8 <= base <= 40:
            g_ref[DEPTH, pl.ds(base + here, 4)] = piece[4:8]
    for piece, at, base in (
        (other_c, 0, 24), (other_1, 0, 16), (other_1, 8, 32),
        (other_23, 0, 8), (other_23, 8, 40), (other_23, 16, 0), (other_23, 20, 48),
    ):
        h_ref[0, pl.ds(base + there, 4)] = piece[at:at + 4]
        if 8 <= base <= 40:
            g_ref[DEPTH, pl.ds(base + there, 4)] = piece[at + 4:at + 8]

    lane = lax.broadcasted_iota(jnp.int32, (128, WID), 1)
    not_first = lane > 0
    not_last = lane < WID - 1
    lane1 = lax.broadcasted_iota(jnp.int32, (1, WID), 1)
    keep_first = (lane1 > 0).astype(F32).astype(BF)
    keep_last = (lane1 < WID - 1).astype(F32).astype(BF)

    def inside(row):
        at = row - OFF + first_row
        return jnp.logical_and(at >= 0, at < ROWS)

    def conv_rows(row, count, source, slab, finish):
        rows = source[pl.ds(row - 1, count + 2)].reshape((count + 2) * C, WID)
        before = pltpu.roll(rows, 1, 1) * keep_first
        after = pltpu.roll(rows, WID - 1, 1) * keep_last
        products = []
        for at in range(0, count, 4):
            halves = []
            for part in (at, at + 2):
                cut = slice(part * C, (part + 4) * C)
                halves.append(jnp.concatenate([before[cut], rows[cut], after[cut]], axis=0))
            products.append(lax.dot_general(
                slab[...],
                jnp.concatenate(halves, axis=1),
                (((1,), (0,)), ((), ())),
                preferred_element_type=F32,
            ))
        for at, product in zip(range(0, count, 4), products):
            for half in range(2):
                for one in range(2):
                    finish(row + at + 2 * half + one, product[one * C:(one + 1) * C, half * WID:(half + 1) * WID])

    def conv_loop(reach, source, slab, finish):
        start = OFF - reach
        count = -(-(8 + 2 * reach) // 4) * 4
        parts = -(-count // 28)
        size = -(-count // (4 * parts)) * 4
        for part in range(parts):
            @pl.when(mine >= 0)
            def _(part=part):
                conv_rows(start + size * part, min(size, count - size * part), source, slab, finish)

    def tangent_of(values):
        return jnp.tanh(values * (gelu_scale + (gelu_scale * cubic_coef) * (values * values)))

    def slope_of(values):
        square = values * values
        tangent = jnp.tanh(values * (gelu_scale + (gelu_scale * cubic_coef) * square))
        return 0.5 * (1.0 + tangent) + (0.5 * values) * (1.0 - tangent * tangent) * (
            gelu_scale + (3.0 * gelu_scale * cubic_coef) * square
        )

    def forward(section, carry):
        def activate(pre_ref, act_ref):
            def finish(row, values):
                pre_ref[section, row] = values
                half = 0.5 * values
                act = half + half * tangent_of(values)
                act_ref[section, row] = jnp.where(inside(row), act, 0.0).astype(BF)

            return finish

        def residual(row, values):
            result = h_ref[section, row].astype(F32) + values
            h_ref[section + 1, row] = jnp.where(inside(row), result, 0.0).astype(BF)

        slot = section * 3
        conv_loop(21 - 3 * section, h_ref.at[section], wf_ref.at[slot],
                  activate(p1_ref, a1_ref))
        conv_loop(20 - 3 * section, a1_ref.at[section], wf_ref.at[slot + 1],
                  activate(p2_ref, a2_ref))
        conv_loop(0 if section == DEPTH - 1 else 19 - 3 * section, a2_ref.at[section],
                  wf_ref.at[slot + 2], residual)
        return carry

    for section in range(DEPTH):
        forward(section, 0)

    def kernel_grad(layer, source, grads):
        wide_in, wide_out = [], []
        for row in range(OFF, OFF + OWN):
            wide_in.append(source[pl.ds(row - 1, 3)].reshape(3 * C, WID))
            out = grads[row].astype(F32)
            after = jnp.where(not_last[:C], pltpu.roll(out, WID - 1, 1), 0.0)
            before = jnp.where(not_first[:C], pltpu.roll(out, 1, 1), 0.0)
            wide_out.append(jnp.concatenate([after, out, before], axis=0).astype(BF))
        result = lax.dot_general(
            jnp.concatenate(wide_in, axis=1),
            jnp.concatenate(wide_out, axis=1),
            (((1,), (1,)), ((), ())),
            preferred_element_type=F32,
        )
        for kw in range(3):
            part = result[:, kw * C:(kw + 1) * C]
            packed = jnp.concatenate([part[:96], part[96:]], axis=1)
            wg_ref[pl.ds((layer * 3 + kw) * 96, 96), :] = packed.astype(BF)

    wg_ref[864:1024, :] = jnp.zeros((160, 128), BF)

    def backward(turn, carry):
        section = DEPTH - 1 - turn
        slot = section * 3

        def through(pre_ref, target):
            def finish(row, values):
                result = values * slope_of(pre_ref[section, row])
                target[section, row] = jnp.where(inside(row), result, 0.0).astype(BF)

            return finish

        def residual(row, values):
            result = g_ref[section + 1, row].astype(F32) + values
            g_ref[section, row] = jnp.where(inside(row), result, 0.0).astype(BF)

        conv_loop(2 + 3 * section, g_ref.at[section + 1], wb_ref.at[slot + 2], through(p2_ref, gp2_ref))
        conv_loop(1 + 3 * section, gp2_ref.at[section], wb_ref.at[slot + 1], through(p1_ref, gp1_ref))

        conv_loop(3 * section, gp1_ref.at[section], wb_ref.at[slot], residual)
        return carry

    for turn in range(DEPTH):
        backward(turn, 0)

    kernel_grad(2, a2_ref.at[mine], g_ref.at[mine + 1])
    kernel_grad(1, a1_ref.at[mine], gp2_ref.at[mine])
    kernel_grad(0, h_ref.at[mine], gp1_ref.at[mine])

    side = where_ref[3]
    kept = OFF + 4 * side
    sent = OFF + 4 * (1 - side)
    even_ref[0] = h_ref[mine + 1, pl.ds(kept, 4)]
    even_ref[1] = g_ref[mine, pl.ds(kept, 4)]
    odd_ref[0] = h_ref[mine + 1, pl.ds(sent, 4)]
    odd_ref[1] = g_ref[mine, pl.ds(sent, 4)]


def unpack_kernel(sum_ref, out_ref):
    for layer in range(3):
        for kw in range(3):
            base = (layer * 3 + kw) * 96
            block = sum_ref[base:base + 96, :].astype(F32)
            tall = jnp.concatenate([block[:, :C], block[:, C:]], axis=0)
            for kh in range(3):
                out_ref[0, layer, kh, kw] = tall[kh * C:(kh + 1) * C]


def vmem(count):
    return [pl.BlockSpec(memory_space=pltpu.VMEM)] * count


def sections_call(where, pieces, fwd, bwd):
    window = (WINDOW, C, WID)
    return pl.pallas_call(
        sections_kernel,
        out_shape=[
            jax.ShapeDtypeStruct((2, 4, C, WID), BF),
            jax.ShapeDtypeStruct((2, 4, C, WID), BF),
            jax.ShapeDtypeStruct((1024, 128), BF),
        ],
        in_specs=[pl.BlockSpec(memory_space=pltpu.SMEM)] + vmem(12),
        out_specs=vmem(3),
        scratch_shapes=[
            pltpu.VMEM((DEPTH + 1,) + window, BF),
            pltpu.VMEM((DEPTH,) + window, BF),
            pltpu.VMEM((DEPTH,) + window, BF),
            pltpu.VMEM((DEPTH,) + window, F32),
            pltpu.VMEM((DEPTH,) + window, F32),
            pltpu.VMEM((DEPTH + 1,) + window, BF),
            pltpu.VMEM((DEPTH,) + window, BF),
            pltpu.VMEM((DEPTH,) + window, BF),
        ],
        compiler_params=pltpu.CompilerParams(vmem_limit_bytes=62 * 1024 * 1024),
        name="sections",
    )(where, *pieces, fwd, bwd)


SECTION = ("pair", "side")
BAND = ("z", "core")
CHIPS = 8


def on_device(images, weights, cotangent):
    pair, side = lax.axis_index("pair"), lax.axis_index("side")
    z, core = lax.axis_index("z"), lax.axis_index("core")
    section = 2 * pair + side
    where = jnp.stack([2 * pair + core, z * OWN, core, side, section]).astype(jnp.int32)

    raw = weights.reshape(27, 2, 32, C)
    raw = jnp.concatenate([raw[:, 0], raw[:, 1]], axis=-1).reshape(864, 128)
    near = lax.ppermute(
        raw,
        SECTION + ("core",),
        [
            (s * 2 + c, (s + 1 - 2 * c) % DEPTH * 2 + c)
            for s in range(DEPTH)
            for c in range(2)
        ],
    )
    half = lax.ppermute(
        jnp.where(core == 0, raw[:448], raw[416:]),
        SECTION,
        [(s, (s + 2) % DEPTH) for s in range(DEPTH)],
    )
    field = jnp.where(side == 0, jnp.stack([images[0], cotangent[0]]), jnp.stack([images[1], cotangent[1]]))
    center = field.transpose(0, 2, 1, 3).reshape(8, C, WID)
    swapped = [(i, i ^ 1) for i in range(2 * CHIPS)]

    def chips_away(value, chips):
        pairs = [(i, i + chips) for i in range(CHIPS) if 0 <= i + chips < CHIPS]
        return lax.ppermute(value, "z", pairs)

    other_c = lax.ppermute(center, BAND, swapped)
    center, other_c, raw = lax.optimization_barrier((center, other_c, raw))
    left3, right3 = chips_away(center[0:4], 3), chips_away(center[0:4], -3)
    left2, right2 = chips_away(center, 2), chips_away(center, -2)
    left1, right1 = chips_away(center, 1), chips_away(center, -1)
    other_1 = lax.ppermute(jnp.concatenate([left1, right1]), BAND, swapped)
    other_23 = lax.ppermute(jnp.concatenate([left2, right2, left3, right3]), BAND, swapped)

    other_weights = lax.ppermute(jnp.concatenate([near, half]), BAND, swapped)
    fwd, bwd = pl.pallas_call(
        weight_blocks_kernel,
        out_shape=[jax.ShapeDtypeStruct((12, 128, 768), BF)] * 2,
        in_specs=[pl.BlockSpec(memory_space=pltpu.SMEM)] + vmem(4),
        out_specs=vmem(2),
        scratch_shapes=[pltpu.VMEM((864, 128), BF)],
        name="weight_blocks",
    )(where, raw, near, half, other_weights)

    even, odd, grads = sections_call(
        where,
        (center, left1, right1, left2, right2, left3, right3, other_c, other_1, other_23),
        fwd,
        bwd,
    )

    parts = lax.all_to_all(grads.reshape(64, 16, 128), ("rep", "side", "z"), 0, 0, tiled=True)
    total = jnp.sum(parts.astype(F32), axis=0).astype(BF)
    turned = [(2 * q + c, 2 * c + q) for q in range(2) for c in range(2)]
    total = lax.ppermute(total, ("side", "core"), turned)
    summed = lax.all_to_all(
        jnp.broadcast_to(total[None], (64, 16, 128)), ("rep", "core", "z"), 0, 0, tiled=True
    ).reshape(1024, 128)

    even = lax.ppermute(even, ("side", "core"), turned)
    odd = lax.ppermute(
        odd, ("side", "core"), [(2 * q + c, 2 * c + 1 - q) for q in range(2) for c in range(2)]
    )
    zero = jnp.where(core == 0, even, odd)
    one = jnp.where(core == 0, odd, even)
    both = jnp.stack([zero, one]).transpose(1, 0, 3, 2, 4)

    weight_grads = pl.pallas_call(
        unpack_kernel,
        out_shape=jax.ShapeDtypeStruct((1, 3, 3, 3, C, C), F32),
        in_specs=vmem(1),
        out_specs=pl.BlockSpec(memory_space=pltpu.VMEM),
        name="unpack",
    )(summed)
    return both[0][None], both[1][None], weight_grads


def solution(mesh):
    finer = Mesh(
        mesh.devices.reshape(2, 2, CHIPS, 2, mesh.devices.shape[2]), SECTION + BAND + ("rep",)
    )
    in_specs = (
        P("rep", None, BAND, None),
        P(SECTION, None, None, None, None, None),
        P("rep", None, BAND, None),
    )
    out_specs = (
        P(SECTION, "rep", None, BAND, None),
        P(SECTION, "rep", None, BAND, None),
        P(SECTION, None, None, None, None, None),
    )
    return jax.shard_map(
        on_device, mesh=finer, in_specs=in_specs, out_specs=out_specs, check_vma=False
    )
```

```python
import jax
import jax.numpy as jnp
from jax import lax
from jax.experimental import pallas as pl
from jax.experimental.pallas import tpu as pltpu
from jax.sharding import Mesh
from jax.sharding import PartitionSpec as P

BF = jnp.bfloat16
F32 = jnp.float32
gelu_scale = 0.7978845608028654
cubic_coef = 0.044715

C = 64
WID = 128
ROWS = 64
OWN = 8
OFF = 24
WINDOW = 56
DEPTH = 4


def weight_blocks_kernel(where_ref, own, near, half, other, fwd_ref, bwd_ref, far):
    zero = jnp.zeros((C, C), BF)
    same = (
        lax.broadcasted_iota(jnp.int32, (C, C), 0) == lax.broadcasted_iota(jnp.int32, (C, C), 1)
    ).astype(F32).astype(BF)
    core = where_ref[2]
    far[pl.ds(pl.multiple_of(416 * core, 32), 448), :] = half[...]
    far[pl.ds(pl.multiple_of(416 * (1 - core), 32), 448), :] = other[864:1312, :]
    for piece, hop in ((own, 0), (near, 1 + 2 * core), (other, 3 - 2 * core), (far, 2)):
        section = lax.rem(where_ref[4] - hop + DEPTH, DEPTH)
        for layer in range(3):
            slot = section * 3 + layer
            for kw in range(3):
                taps = []
                for kh in range(3):
                    at = layer * 288 + (kh * 3 + kw) * 32
                    block = piece[at:at + 32, :]
                    taps.append(jnp.concatenate([block[:, :C], block[:, C:]], axis=0))
                tall = jnp.concatenate(taps + [zero] + [zero] + taps, axis=0)
                flat = lax.dot_general(
                    same, tall, (((1,), (1,)), ((), ())), preferred_element_type=F32
                ).astype(BF)
                here = slice(kw * 256, kw * 256 + 256)
                fwd_ref[slot, 0:C, here] = flat[:, 0:256]
                fwd_ref[slot, C:2 * C, here] = flat[:, 256:512]
                there = (2 - kw) * 256
                left = jnp.concatenate([taps[2], taps[1]], axis=1)
                middle = jnp.concatenate([taps[1], taps[0]], axis=1)
                bwd_ref[slot, 0:C, there:there + 128] = left
                bwd_ref[slot, 0:C, there + 128:there + 256] = jnp.concatenate([taps[0], zero], axis=1)
                bwd_ref[slot, C:2 * C, there:there + 128] = jnp.concatenate([zero, taps[2]], axis=1)
                bwd_ref[slot, C:2 * C, there + 128:there + 256] = middle


def sections_kernel(
    where_ref,
    chip_rows, got1, got2, got3, other1, other2, other3,
    wf_ref, wb_ref,
    even_ref, odd_ref, wg_ref,
    h_ref, a1_ref, a2_ref, p1_ref, p2_ref, g_ref, gp1_ref, gp2_ref,
):
    mine = where_ref[0]
    first_row = where_ref[1]
    core = where_ref[2]
    h_ref[0, 24:32] = chip_rows[0:8]
    g_ref[DEPTH, 24:32] = chip_rows[8:16]
    for pieces, lower in (((got1, got2, got3), core), ((other1, other2, other3), 1 - core)):
        one, two, three = pieces
        h_ref[0, pl.ds(16 + 16 * lower, 8)] = one[0:8]
        h_ref[0, pl.ds(8 + 32 * lower, 8)] = two[0:8]
        h_ref[0, pl.ds(2 + 46 * lower, 6)] = three[...]
        g_ref[DEPTH, pl.ds(16 + 16 * lower, 8)] = one[8:16]
        g_ref[DEPTH, pl.ds(12 + 28 * lower, 4)] = two[8:12]

    lane = lax.broadcasted_iota(jnp.int32, (128, WID), 1)
    not_first = lane > 0
    not_last = lane < WID - 1
    lane1 = lax.broadcasted_iota(jnp.int32, (1, WID), 1)
    keep_first = (lane1 > 0).astype(F32).astype(BF)
    keep_last = (lane1 < WID - 1).astype(F32).astype(BF)

    def inside(row):
        at = row - OFF + first_row
        return jnp.logical_and(at >= 0, at < ROWS)

    def conv_rows(row, count, source, slab, finish):
        rows = source[pl.ds(row - 1, count + 2)].reshape((count + 2) * C, WID)
        before = pltpu.roll(rows, 1, 1) * keep_first
        after = pltpu.roll(rows, WID - 1, 1) * keep_last
        products = []
        for at in range(0, count, 4):
            halves = []
            for part in (at, at + 2):
                cut = slice(part * C, (part + 4) * C)
                halves.append(jnp.concatenate([before[cut], rows[cut], after[cut]], axis=0))
            products.append(lax.dot_general(
                slab[...],
                jnp.concatenate(halves, axis=1),
                (((1,), (0,)), ((), ())),
                preferred_element_type=F32,
            ))
        for at, product in zip(range(0, count, 4), products):
            for half in range(2):
                for one in range(2):
                    finish(row + at + 2 * half + one, product[one * C:(one + 1) * C, half * WID:(half + 1) * WID])

    def conv_loop(reach, source, slab, finish):
        start = OFF - reach
        count = -(-(8 + 2 * reach) // 4) * 4
        parts = -(-count // 28)
        size = -(-count // (4 * parts)) * 4
        for part in range(parts):
            @pl.when(mine >= 0)
            def _(part=part):
                conv_rows(start + size * part, min(size, count - size * part), source, slab, finish)

    def tangent_of(values):
        return jnp.tanh(values * (gelu_scale + (gelu_scale * cubic_coef) * (values * values)))

    def slope_of(values):
        square = values * values
        tangent = jnp.tanh(values * (gelu_scale + (gelu_scale * cubic_coef) * square))
        return 0.5 * (1.0 + tangent) + (0.5 * values) * (1.0 - tangent * tangent) * (
            gelu_scale + (3.0 * gelu_scale * cubic_coef) * square
        )

    def forward(section, carry):
        def activate(pre_ref, act_ref):
            def finish(row, values):
                pre_ref[section, row] = values
                half = 0.5 * values
                act = half + half * tangent_of(values)
                act_ref[section, row] = jnp.where(inside(row), act, 0.0).astype(BF)

            return finish

        def residual(row, values):
            result = h_ref[section, row].astype(F32) + values
            h_ref[section + 1, row] = jnp.where(inside(row), result, 0.0).astype(BF)

        slot = section * 3
        conv_loop(21 - 3 * section, h_ref.at[section], wf_ref.at[slot],
                  activate(p1_ref, a1_ref))
        conv_loop(20 - 3 * section, a1_ref.at[section], wf_ref.at[slot + 1],
                  activate(p2_ref, a2_ref))
        conv_loop(0 if section == DEPTH - 1 else 19 - 3 * section, a2_ref.at[section],
                  wf_ref.at[slot + 2], residual)
        return carry

    for section in range(DEPTH):
        forward(section, 0)

    def kernel_grad(layer, source, grads):
        wide_in, wide_out = [], []
        for row in range(OFF, OFF + OWN):
            wide_in.append(source[pl.ds(row - 1, 3)].reshape(3 * C, WID))
            out = grads[row].astype(F32)
            after = jnp.where(not_last[:C], pltpu.roll(out, WID - 1, 1), 0.0)
            before = jnp.where(not_first[:C], pltpu.roll(out, 1, 1), 0.0)
            wide_out.append(jnp.concatenate([after, out, before], axis=0).astype(BF))
        result = lax.dot_general(
            jnp.concatenate(wide_in, axis=1),
            jnp.concatenate(wide_out, axis=1),
            (((1,), (1,)), ((), ())),
            preferred_element_type=F32,
        )
        for kw in range(3):
            part = result[:, kw * C:(kw + 1) * C]
            packed = jnp.concatenate([part[:96], part[96:]], axis=1)
            wg_ref[pl.ds((layer * 3 + kw) * 96, 96), :] = packed.astype(BF)

    wg_ref[864:1024, :] = jnp.zeros((160, 128), BF)

    def backward(turn, carry):
        section = DEPTH - 1 - turn
        slot = section * 3

        def through(pre_ref, target):
            def finish(row, values):
                result = values * slope_of(pre_ref[section, row])
                target[section, row] = jnp.where(inside(row), result, 0.0).astype(BF)

            return finish

        def residual(row, values):
            result = g_ref[section + 1, row].astype(F32) + values
            g_ref[section, row] = jnp.where(inside(row), result, 0.0).astype(BF)

        conv_loop(2 + 3 * section, g_ref.at[section + 1], wb_ref.at[slot + 2], through(p2_ref, gp2_ref))
        conv_loop(1 + 3 * section, gp2_ref.at[section], wb_ref.at[slot + 1], through(p1_ref, gp1_ref))

        conv_loop(3 * section, gp1_ref.at[section], wb_ref.at[slot], residual)
        return carry

    for turn in range(DEPTH):
        backward(turn, 0)

    kernel_grad(2, a2_ref.at[mine], g_ref.at[mine + 1])
    kernel_grad(1, a1_ref.at[mine], gp2_ref.at[mine])
    kernel_grad(0, h_ref.at[mine], gp1_ref.at[mine])

    side = where_ref[3]
    kept = OFF + 4 * side
    sent = OFF + 4 * (1 - side)
    even_ref[0] = h_ref[mine + 1, pl.ds(kept, 4)]
    even_ref[1] = g_ref[mine, pl.ds(kept, 4)]
    odd_ref[0] = h_ref[mine + 1, pl.ds(sent, 4)]
    odd_ref[1] = g_ref[mine, pl.ds(sent, 4)]


def unpack_kernel(sum_ref, out_ref):
    for layer in range(3):
        for kw in range(3):
            base = (layer * 3 + kw) * 96
            block = sum_ref[base:base + 96, :].astype(F32)
            tall = jnp.concatenate([block[:, :C], block[:, C:]], axis=0)
            for kh in range(3):
                out_ref[0, layer, kh, kw] = tall[kh * C:(kh + 1) * C]


def vmem(count):
    return [pl.BlockSpec(memory_space=pltpu.VMEM)] * count


def sections_call(where, pieces, fwd, bwd):
    window = (WINDOW, C, WID)
    return pl.pallas_call(
        sections_kernel,
        out_shape=[
            jax.ShapeDtypeStruct((2, 4, C, WID), BF),
            jax.ShapeDtypeStruct((2, 4, C, WID), BF),
            jax.ShapeDtypeStruct((1024, 128), BF),
        ],
        in_specs=[pl.BlockSpec(memory_space=pltpu.SMEM)] + vmem(9),
        out_specs=vmem(3),
        scratch_shapes=[
            pltpu.VMEM((DEPTH + 1,) + window, BF),
            pltpu.VMEM((DEPTH,) + window, BF),
            pltpu.VMEM((DEPTH,) + window, BF),
            pltpu.VMEM((DEPTH,) + window, F32),
            pltpu.VMEM((DEPTH,) + window, F32),
            pltpu.VMEM((DEPTH + 1,) + window, BF),
            pltpu.VMEM((DEPTH,) + window, BF),
            pltpu.VMEM((DEPTH,) + window, BF),
        ],
        compiler_params=pltpu.CompilerParams(vmem_limit_bytes=62 * 1024 * 1024),
        name="sections",
    )(where, *pieces, fwd, bwd)


SECTION = ("pair", "side")
BAND = ("z", "core")
CHIPS = 8


def on_device(images, weights, cotangent):
    pair, side = lax.axis_index("pair"), lax.axis_index("side")
    z, core = lax.axis_index("z"), lax.axis_index("core")
    section = 2 * pair + side
    where = jnp.stack([2 * pair + core, z * OWN, core, side, section]).astype(jnp.int32)

    raw = weights.reshape(27, 2, 32, C)
    raw = jnp.concatenate([raw[:, 0], raw[:, 1]], axis=-1).reshape(864, 128)
    near = lax.ppermute(
        raw,
        SECTION + ("core",),
        [
            (s * 2 + c, (s + 1 - 2 * c) % DEPTH * 2 + c)
            for s in range(DEPTH)
            for c in range(2)
        ],
    )
    half = lax.ppermute(
        jnp.where(core == 0, raw[:448], raw[416:]),
        SECTION,
        [(s, (s + 2) % DEPTH) for s in range(DEPTH)],
    )
    field = jnp.where(side == 0, jnp.stack([images[0], cotangent[0]]), jnp.stack([images[1], cotangent[1]]))
    center = field.transpose(0, 2, 1, 3).reshape(8, C, WID)
    swapped = [(i, i ^ 1) for i in range(2 * CHIPS)]

    def chips_away(value, chips):
        pairs = [
            (2 * z + c, 2 * (z + step) + c)
            for c, step in ((0, chips), (1, -chips))
            for z in range(CHIPS)
            if 0 <= z + step < CHIPS
        ]
        return lax.ppermute(value, BAND, pairs)

    upper = core == 0
    swap = lax.ppermute(center, BAND, swapped)
    first, last = jnp.where(upper, center, swap), jnp.where(upper, swap, center)
    chip = jnp.concatenate([first[0:4], last[0:4], first[4:8], last[4:8]])
    got3 = chips_away(jnp.where(upper, chip[2:8], chip[0:6]), 3)
    got2 = chips_away(jnp.concatenate([chip[0:8], jnp.where(upper, chip[12:16], chip[8:12])]), 2)
    got1 = chips_away(chip, 1)
    other1, other2, other3 = (lax.ppermute(got, BAND, swapped) for got in (got1, got2, got3))
    other_weights = lax.ppermute(jnp.concatenate([near, half]), BAND, swapped)
    fwd, bwd = pl.pallas_call(
        weight_blocks_kernel,
        out_shape=[jax.ShapeDtypeStruct((12, 128, 768), BF)] * 2,
        in_specs=[pl.BlockSpec(memory_space=pltpu.SMEM)] + vmem(4),
        out_specs=vmem(2),
        scratch_shapes=[pltpu.VMEM((864, 128), BF)],
        name="weight_blocks",
    )(where, raw, near, half, other_weights)

    even, odd, grads = sections_call(
        where,
        (chip, got1, got2, got3, other1, other2, other3),
        fwd,
        bwd,
    )

    parts = lax.all_to_all(grads.reshape(64, 16, 128), ("rep", "side", "z"), 0, 0, tiled=True)
    total = jnp.sum(parts.astype(F32), axis=0).astype(BF)
    turned = [(2 * q + c, 2 * c + q) for q in range(2) for c in range(2)]
    total = lax.ppermute(total, ("side", "core"), turned)
    summed = lax.all_to_all(
        jnp.broadcast_to(total[None], (64, 16, 128)), ("rep", "core", "z"), 0, 0, tiled=True
    ).reshape(1024, 128)

    even = lax.ppermute(even, ("side", "core"), turned)
    odd = lax.ppermute(
        odd, ("side", "core"), [(2 * q + c, 2 * c + 1 - q) for q in range(2) for c in range(2)]
    )
    zero = jnp.where(core == 0, even, odd)
    one = jnp.where(core == 0, odd, even)
    both = jnp.stack([zero, one]).transpose(1, 0, 3, 2, 4)

    weight_grads = pl.pallas_call(
        unpack_kernel,
        out_shape=jax.ShapeDtypeStruct((1, 3, 3, 3, C, C), F32),
        in_specs=vmem(1),
        out_specs=pl.BlockSpec(memory_space=pltpu.VMEM),
        name="unpack",
    )(summed)
    return both[0][None], both[1][None], weight_grads


def solution(mesh):
    finer = Mesh(
        mesh.devices.reshape(2, 2, CHIPS, 2, mesh.devices.shape[2]), SECTION + BAND + ("rep",)
    )
    in_specs = (
        P("rep", None, BAND, None),
        P(SECTION, None, None, None, None, None),
        P("rep", None, BAND, None),
    )
    out_specs = (
        P(SECTION, "rep", None, BAND, None),
        P(SECTION, "rep", None, BAND, None),
        P(SECTION, None, None, None, None, None),
    )
    return jax.shard_map(
        on_device, mesh=finer, in_specs=in_specs, out_specs=out_specs, check_vma=False
    )
```

```python
import jax
import jax.numpy as jnp
from jax import lax
from jax.experimental import pallas as pl
from jax.experimental.pallas import tpu as pltpu
from jax.sharding import Mesh
from jax.sharding import PartitionSpec as P

BF = jnp.bfloat16
F32 = jnp.float32
gelu_scale = 0.7978845608028654
cubic_coef = 0.044715

C = 64
WID = 128
ROWS = 64
OWN = 8
OFF = 24
WINDOW = 56
DEPTH = 4


def weight_blocks_kernel(where_ref, own, near, half, other, fwd_ref, bwd_ref, far):
    zero = jnp.zeros((C, C), BF)
    same = (
        lax.broadcasted_iota(jnp.int32, (C, C), 0) == lax.broadcasted_iota(jnp.int32, (C, C), 1)
    ).astype(F32).astype(BF)
    core = where_ref[2]
    far[pl.ds(pl.multiple_of(416 * core, 32), 448), :] = half[...]
    far[pl.ds(pl.multiple_of(416 * (1 - core), 32), 448), :] = other[864:1312, :]
    for piece, hop in ((own, 0), (near, 1 + 2 * core), (other, 3 - 2 * core), (far, 2)):
        section = lax.rem(where_ref[4] - hop + DEPTH, DEPTH)
        for layer in range(3):
            slot = section * 3 + layer
            for kw in range(3):
                taps = []
                for kh in range(3):
                    at = layer * 288 + (kh * 3 + kw) * 32
                    block = piece[at:at + 32, :]
                    taps.append(jnp.concatenate([block[:, :C], block[:, C:]], axis=0))
                tall = jnp.concatenate(taps + [zero] + [zero] + taps, axis=0)
                flat = lax.dot_general(
                    same, tall, (((1,), (1,)), ((), ())), preferred_element_type=F32
                ).astype(BF)
                here = slice(kw * 256, kw * 256 + 256)
                fwd_ref[slot, 0:C, here] = flat[:, 0:256]
                fwd_ref[slot, C:2 * C, here] = flat[:, 256:512]
                there = (2 - kw) * 256
                left = jnp.concatenate([taps[2], taps[1]], axis=1)
                middle = jnp.concatenate([taps[1], taps[0]], axis=1)
                bwd_ref[slot, 0:C, there:there + 128] = left
                bwd_ref[slot, 0:C, there + 128:there + 256] = jnp.concatenate([taps[0], zero], axis=1)
                bwd_ref[slot, C:2 * C, there:there + 128] = jnp.concatenate([zero, taps[2]], axis=1)
                bwd_ref[slot, C:2 * C, there + 128:there + 256] = middle


def sections_kernel(
    where_ref,
    chip_rows, near_rows, far_rows, other_near, other_far,
    wf_ref, wb_ref,
    even_ref, odd_ref, wg_ref,
    h_ref, a1_ref, a2_ref, p1_ref, p2_ref, g_ref, gp1_ref, gp2_ref,
):
    mine = where_ref[0]
    first_row = where_ref[1]
    core = where_ref[2]
    h_ref[0, 24:32] = chip_rows[0:8]
    g_ref[DEPTH, 24:32] = chip_rows[8:16]
    for one, two, lower in ((near_rows, far_rows, core), (other_near, other_far, 1 - core)):
        h_ref[0, pl.ds(16 + 16 * lower, 8)] = one[0:8]
        h_ref[0, pl.ds(2 + 38 * lower, 14)] = two[0:14]
        g_ref[DEPTH, pl.ds(16 + 16 * lower, 8)] = one[8:16]
        g_ref[DEPTH, pl.ds(12 + 28 * lower, 4)] = two[14:18]

    lane = lax.broadcasted_iota(jnp.int32, (128, WID), 1)
    not_first = lane > 0
    not_last = lane < WID - 1
    lane1 = lax.broadcasted_iota(jnp.int32, (1, WID), 1)
    keep_first = (lane1 > 0).astype(F32).astype(BF)
    keep_last = (lane1 < WID - 1).astype(F32).astype(BF)

    def inside(row):
        at = row - OFF + first_row
        return jnp.logical_and(at >= 0, at < ROWS)

    def conv_rows(row, count, source, slab, finish):
        rows = source[pl.ds(row - 1, count + 2)].reshape((count + 2) * C, WID)
        before = pltpu.roll(rows, 1, 1) * keep_first
        after = pltpu.roll(rows, WID - 1, 1) * keep_last
        products = []
        for at in range(0, count, 4):
            halves = []
            for part in (at, at + 2):
                cut = slice(part * C, (part + 4) * C)
                halves.append(jnp.concatenate([before[cut], rows[cut], after[cut]], axis=0))
            products.append(lax.dot_general(
                slab[...],
                jnp.concatenate(halves, axis=1),
                (((1,), (0,)), ((), ())),
                preferred_element_type=F32,
            ))
        for at, product in zip(range(0, count, 4), products):
            for half in range(2):
                for one in range(2):
                    finish(row + at + 2 * half + one, product[one * C:(one + 1) * C, half * WID:(half + 1) * WID])

    def conv_loop(reach, source, slab, finish):
        start = OFF - reach
        count = -(-(8 + 2 * reach) // 4) * 4
        parts = -(-count // 28)
        size = -(-count // (4 * parts)) * 4
        for part in range(parts):
            @pl.when(mine >= 0)
            def _(part=part):
                conv_rows(start + size * part, min(size, count - size * part), source, slab, finish)

    def tangent_of(values):
        return jnp.tanh(values * (gelu_scale + (gelu_scale * cubic_coef) * (values * values)))

    def slope_of(values):
        square = values * values
        tangent = jnp.tanh(values * (gelu_scale + (gelu_scale * cubic_coef) * square))
        return 0.5 * (1.0 + tangent) + (0.5 * values) * (1.0 - tangent * tangent) * (
            gelu_scale + (3.0 * gelu_scale * cubic_coef) * square
        )

    def forward(section, carry):
        def activate(pre_ref, act_ref):
            def finish(row, values):
                pre_ref[section, row] = values
                half = 0.5 * values
                act = half + half * tangent_of(values)
                act_ref[section, row] = jnp.where(inside(row), act, 0.0).astype(BF)

            return finish

        def residual(row, values):
            result = h_ref[section, row].astype(F32) + values
            h_ref[section + 1, row] = jnp.where(inside(row), result, 0.0).astype(BF)

        slot = section * 3
        conv_loop(21 - 3 * section, h_ref.at[section], wf_ref.at[slot],
                  activate(p1_ref, a1_ref))
        conv_loop(20 - 3 * section, a1_ref.at[section], wf_ref.at[slot + 1],
                  activate(p2_ref, a2_ref))
        conv_loop(0 if section == DEPTH - 1 else 19 - 3 * section, a2_ref.at[section],
                  wf_ref.at[slot + 2], residual)
        return carry

    for section in range(DEPTH):
        forward(section, 0)

    def kernel_grad(layer, source, grads):
        wide_in, wide_out = [], []
        for row in range(OFF, OFF + OWN):
            wide_in.append(source[pl.ds(row - 1, 3)].reshape(3 * C, WID))
            out = grads[row].astype(F32)
            after = jnp.where(not_last[:C], pltpu.roll(out, WID - 1, 1), 0.0)
            before = jnp.where(not_first[:C], pltpu.roll(out, 1, 1), 0.0)
            wide_out.append(jnp.concatenate([after, out, before], axis=0).astype(BF))
        result = lax.dot_general(
            jnp.concatenate(wide_in, axis=1),
            jnp.concatenate(wide_out, axis=1),
            (((1,), (1,)), ((), ())),
            preferred_element_type=F32,
        )
        for kw in range(3):
            part = result[:, kw * C:(kw + 1) * C]
            packed = jnp.concatenate([part[:96], part[96:]], axis=1)
            wg_ref[pl.ds((layer * 3 + kw) * 96, 96), :] = packed.astype(BF)

    wg_ref[864:1024, :] = jnp.zeros((160, 128), BF)

    def backward(turn, carry):
        section = DEPTH - 1 - turn
        slot = section * 3

        def through(pre_ref, target):
            def finish(row, values):
                result = values * slope_of(pre_ref[section, row])
                target[section, row] = jnp.where(inside(row), result, 0.0).astype(BF)

            return finish

        def residual(row, values):
            result = g_ref[section + 1, row].astype(F32) + values
            g_ref[section, row] = jnp.where(inside(row), result, 0.0).astype(BF)

        conv_loop(2 + 3 * section, g_ref.at[section + 1], wb_ref.at[slot + 2], through(p2_ref, gp2_ref))
        conv_loop(1 + 3 * section, gp2_ref.at[section], wb_ref.at[slot + 1], through(p1_ref, gp1_ref))

        conv_loop(3 * section, gp1_ref.at[section], wb_ref.at[slot], residual)
        return carry

    for turn in range(DEPTH):
        backward(turn, 0)

    kernel_grad(2, a2_ref.at[mine], g_ref.at[mine + 1])
    kernel_grad(1, a1_ref.at[mine], gp2_ref.at[mine])
    kernel_grad(0, h_ref.at[mine], gp1_ref.at[mine])

    side = where_ref[3]
    kept = OFF + 4 * side
    sent = OFF + 4 * (1 - side)
    even_ref[0] = h_ref[mine + 1, pl.ds(kept, 4)]
    even_ref[1] = g_ref[mine, pl.ds(kept, 4)]
    odd_ref[0] = h_ref[mine + 1, pl.ds(sent, 4)]
    odd_ref[1] = g_ref[mine, pl.ds(sent, 4)]


def unpack_kernel(sum_ref, out_ref):
    for layer in range(3):
        for kw in range(3):
            base = (layer * 3 + kw) * 96
            block = sum_ref[base:base + 96, :].astype(F32)
            tall = jnp.concatenate([block[:, :C], block[:, C:]], axis=0)
            for kh in range(3):
                out_ref[0, layer, kh, kw] = tall[kh * C:(kh + 1) * C]


def vmem(count):
    return [pl.BlockSpec(memory_space=pltpu.VMEM)] * count


def sections_call(where, pieces, fwd, bwd):
    window = (WINDOW, C, WID)
    return pl.pallas_call(
        sections_kernel,
        out_shape=[
            jax.ShapeDtypeStruct((2, 4, C, WID), BF),
            jax.ShapeDtypeStruct((2, 4, C, WID), BF),
            jax.ShapeDtypeStruct((1024, 128), BF),
        ],
        in_specs=[pl.BlockSpec(memory_space=pltpu.SMEM)] + vmem(7),
        out_specs=vmem(3),
        scratch_shapes=[
            pltpu.VMEM((DEPTH + 1,) + window, BF),
            pltpu.VMEM((DEPTH,) + window, BF),
            pltpu.VMEM((DEPTH,) + window, BF),
            pltpu.VMEM((DEPTH,) + window, F32),
            pltpu.VMEM((DEPTH,) + window, F32),
            pltpu.VMEM((DEPTH + 1,) + window, BF),
            pltpu.VMEM((DEPTH,) + window, BF),
            pltpu.VMEM((DEPTH,) + window, BF),
        ],
        compiler_params=pltpu.CompilerParams(vmem_limit_bytes=62 * 1024 * 1024),
        name="sections",
    )(where, *pieces, fwd, bwd)


SECTION = ("pair", "side")
BAND = ("z", "core")
CHIPS = 8


def on_device(images, weights, cotangent):
    pair, side = lax.axis_index("pair"), lax.axis_index("side")
    z, core = lax.axis_index("z"), lax.axis_index("core")
    section = 2 * pair + side
    where = jnp.stack([2 * pair + core, z * OWN, core, side, section]).astype(jnp.int32)

    raw = weights.reshape(27, 2, 32, C)
    raw = jnp.concatenate([raw[:, 0], raw[:, 1]], axis=-1).reshape(864, 128)
    near = lax.ppermute(
        raw,
        SECTION + ("core",),
        [
            (s * 2 + c, (s + 1 - 2 * c) % DEPTH * 2 + c)
            for s in range(DEPTH)
            for c in range(2)
        ],
    )
    half = lax.ppermute(
        jnp.where(core == 0, raw[:448], raw[416:]),
        SECTION,
        [(s, (s + 2) % DEPTH) for s in range(DEPTH)],
    )
    field = jnp.where(side == 0, jnp.stack([images[0], cotangent[0]]), jnp.stack([images[1], cotangent[1]]))
    center = field.transpose(0, 2, 1, 3).reshape(8, C, WID)
    swapped = [(i, i ^ 1) for i in range(2 * CHIPS)]

    def chips_away(value, chips):
        pairs = [
            (2 * z + c, 2 * (z + step) + c)
            for c, step in ((0, chips), (1, -chips))
            for z in range(CHIPS)
            if 0 <= z + step < CHIPS
        ]
        return lax.ppermute(value, BAND, pairs)

    upper = core == 0
    swap = lax.ppermute(center, BAND, swapped)
    first, last = jnp.where(upper, center, swap), jnp.where(upper, swap, center)
    chip = jnp.concatenate([first[0:4], last[0:4], first[4:8], last[4:8]])
    near_rows = chips_away(chip, 1)
    other_near = lax.ppermute(near_rows, BAND, swapped)
    far_rows = chips_away(
        jnp.where(
            upper,
            jnp.concatenate([near_rows[2:8], chip[0:8], chip[12:16]]),
            jnp.concatenate([chip[0:8], near_rows[0:6], chip[8:12]]),
        ),
        2,
    )
    other_weights = lax.ppermute(jnp.concatenate([near, half]), BAND, swapped)
    fwd, bwd = pl.pallas_call(
        weight_blocks_kernel,
        out_shape=[jax.ShapeDtypeStruct((12, 128, 768), BF)] * 2,
        in_specs=[pl.BlockSpec(memory_space=pltpu.SMEM)] + vmem(4),
        out_specs=vmem(2),
        scratch_shapes=[pltpu.VMEM((864, 128), BF)],
        name="weight_blocks",
    )(where, raw, near, half, other_weights)
    far_rows, other_near, fwd, bwd = lax.optimization_barrier((far_rows, other_near, fwd, bwd))
    other_far = lax.ppermute(far_rows, BAND, swapped)

    even, odd, grads = sections_call(
        where,
        (chip, near_rows, far_rows, other_near, other_far),
        fwd,
        bwd,
    )

    parts = lax.all_to_all(grads.reshape(64, 16, 128), ("rep", "side", "z"), 0, 0, tiled=True)
    total = jnp.sum(parts.astype(F32), axis=0).astype(BF)
    turned = [(2 * q + c, 2 * c + q) for q in range(2) for c in range(2)]
    total = lax.ppermute(total, ("side", "core"), turned)
    summed = lax.all_to_all(
        jnp.broadcast_to(total[None], (64, 16, 128)), ("rep", "core", "z"), 0, 0, tiled=True
    ).reshape(1024, 128)

    even = lax.ppermute(even, ("side", "core"), turned)
    odd = lax.ppermute(
        odd, ("side", "core"), [(2 * q + c, 2 * c + 1 - q) for q in range(2) for c in range(2)]
    )
    zero = jnp.where(core == 0, even, odd)
    one = jnp.where(core == 0, odd, even)
    both = jnp.stack([zero, one]).transpose(1, 0, 3, 2, 4)

    weight_grads = pl.pallas_call(
        unpack_kernel,
        out_shape=jax.ShapeDtypeStruct((1, 3, 3, 3, C, C), F32),
        in_specs=vmem(1),
        out_specs=pl.BlockSpec(memory_space=pltpu.VMEM),
        name="unpack",
    )(summed)
    return both[0][None], both[1][None], weight_grads


def solution(mesh):
    finer = Mesh(
        mesh.devices.reshape(2, 2, CHIPS, 2, mesh.devices.shape[2]), SECTION + BAND + ("rep",)
    )
    in_specs = (
        P("rep", None, BAND, None),
        P(SECTION, None, None, None, None, None),
        P("rep", None, BAND, None),
    )
    out_specs = (
        P(SECTION, "rep", None, BAND, None),
        P(SECTION, "rep", None, BAND, None),
        P(SECTION, None, None, None, None, None),
    )
    return jax.shard_map(
        on_device, mesh=finer, in_specs=in_specs, out_specs=out_specs, check_vma=False
    )
```

```python
import jax
import jax.numpy as jnp
from jax import lax
from jax.experimental import pallas as pl
from jax.experimental.pallas import tpu as pltpu
from jax.sharding import Mesh
from jax.sharding import PartitionSpec as P

BF = jnp.bfloat16
F32 = jnp.float32
gelu_scale = 0.7978845608028654
cubic_coef = 0.044715

C = 64
WID = 128
ROWS = 64
OWN = 8
OFF = 24
WINDOW = 56
DEPTH = 4


def weight_blocks_kernel(where_ref, own, near, half, other, fwd_ref, bwd_ref, far):
    zero = jnp.zeros((C, C), BF)
    same = (
        lax.broadcasted_iota(jnp.int32, (C, C), 0) == lax.broadcasted_iota(jnp.int32, (C, C), 1)
    ).astype(F32).astype(BF)
    core = where_ref[2]
    far[pl.ds(pl.multiple_of(416 * core, 32), 448), :] = half[...]
    far[pl.ds(pl.multiple_of(416 * (1 - core), 32), 448), :] = other[864:1312, :]
    for piece, hop in ((own, 0), (near, 1 + 2 * core), (other, 3 - 2 * core), (far, 2)):
        section = lax.rem(where_ref[4] - hop + DEPTH, DEPTH)
        for layer in range(3):
            slot = section * 3 + layer
            for kw in range(3):
                taps = []
                for kh in range(3):
                    at = layer * 288 + (kh * 3 + kw) * 32
                    block = piece[at:at + 32, :]
                    taps.append(jnp.concatenate([block[:, :C], block[:, C:]], axis=0))
                tall = jnp.concatenate(taps + [zero] + [zero] + taps, axis=0)
                flat = lax.dot_general(
                    same, tall, (((1,), (1,)), ((), ())), preferred_element_type=F32
                ).astype(BF)
                here = slice(kw * 256, kw * 256 + 256)
                fwd_ref[slot, 0:C, here] = flat[:, 0:256]
                fwd_ref[slot, C:2 * C, here] = flat[:, 256:512]
                there = (2 - kw) * 256
                left = jnp.concatenate([taps[2], taps[1]], axis=1)
                middle = jnp.concatenate([taps[1], taps[0]], axis=1)
                bwd_ref[slot, 0:C, there:there + 128] = left
                bwd_ref[slot, 0:C, there + 128:there + 256] = jnp.concatenate([taps[0], zero], axis=1)
                bwd_ref[slot, C:2 * C, there:there + 128] = jnp.concatenate([zero, taps[2]], axis=1)
                bwd_ref[slot, C:2 * C, there + 128:there + 256] = middle


def sections_kernel(
    where_ref,
    chip_rows, near_rows, far_rows, other_near, other_far,
    wf_hbm, wb_hbm,
    even_ref, odd_ref, wg_ref,
    h_ref, a1_ref, a2_ref, p1_ref, p2_ref, g_ref, gp1_ref, gp2_ref, wf_ref, wb_ref, sems,
):
    mine = where_ref[0]
    first_row = where_ref[1]
    core = where_ref[2]
    slabs = [
        pltpu.make_async_copy(
            wf_hbm.at[3 * n:3 * n + 3], wf_ref.at[3 * n:3 * n + 3], sems.at[n]
        )
        for n in range(DEPTH)
    ] + [pltpu.make_async_copy(wb_hbm, wb_ref, sems.at[DEPTH])]
    for slab_copy in slabs:
        slab_copy.start()
    h_ref[0, 24:32] = chip_rows[0:8]
    g_ref[DEPTH, 24:32] = chip_rows[8:16]
    for one, two, lower in ((near_rows, far_rows, core), (other_near, other_far, 1 - core)):
        h_ref[0, pl.ds(16 + 16 * lower, 8)] = one[0:8]
        h_ref[0, pl.ds(2 + 38 * lower, 14)] = two[0:14]
        g_ref[DEPTH, pl.ds(16 + 16 * lower, 8)] = one[8:16]
        g_ref[DEPTH, pl.ds(12 + 28 * lower, 4)] = two[14:18]

    lane = lax.broadcasted_iota(jnp.int32, (128, WID), 1)
    not_first = lane > 0
    not_last = lane < WID - 1
    lane1 = lax.broadcasted_iota(jnp.int32, (1, WID), 1)
    keep_first = (lane1 > 0).astype(F32).astype(BF)
    keep_last = (lane1 < WID - 1).astype(F32).astype(BF)

    def inside(row):
        at = row - OFF + first_row
        return jnp.logical_and(at >= 0, at < ROWS)

    def conv_rows(row, count, source, slab, finish):
        rows = source[pl.ds(row - 1, count + 2)].reshape((count + 2) * C, WID)
        before = pltpu.roll(rows, 1, 1) * keep_first
        after = pltpu.roll(rows, WID - 1, 1) * keep_last
        products = []
        for at in range(0, count, 4):
            halves = []
            for part in (at, at + 2):
                cut = slice(part * C, (part + 4) * C)
                halves.append(jnp.concatenate([before[cut], rows[cut], after[cut]], axis=0))
            products.append(lax.dot_general(
                slab[...],
                jnp.concatenate(halves, axis=1),
                (((1,), (0,)), ((), ())),
                preferred_element_type=F32,
            ))
        for at, product in zip(range(0, count, 4), products):
            for half in range(2):
                for one in range(2):
                    finish(row + at + 2 * half + one, product[one * C:(one + 1) * C, half * WID:(half + 1) * WID])

    def conv_loop(reach, source, slab, finish, needed=None):
        start = OFF - reach
        count = -(-(8 + 2 * reach) // 4) * 4
        parts = -(-count // 28)
        size = -(-count // (4 * parts)) * 4
        for part in range(parts):
            @pl.when(mine >= 0 if needed is None else needed)
            def _(part=part):
                conv_rows(start + size * part, min(size, count - size * part), source, slab, finish)

    def tangent_of(values):
        return jnp.tanh(values * (gelu_scale + (gelu_scale * cubic_coef) * (values * values)))

    def slope_of(values):
        square = values * values
        tangent = jnp.tanh(values * (gelu_scale + (gelu_scale * cubic_coef) * square))
        return 0.5 * (1.0 + tangent) + (0.5 * values) * (1.0 - tangent * tangent) * (
            gelu_scale + (3.0 * gelu_scale * cubic_coef) * square
        )

    def forward(section, carry):
        def activate(pre_ref, act_ref):
            def finish(row, values):
                pre_ref[section, row] = values
                half = 0.5 * values
                act = half + half * tangent_of(values)
                act_ref[section, row] = jnp.where(inside(row), act, 0.0).astype(BF)

            return finish

        def residual(row, values):
            result = h_ref[section, row].astype(F32) + values
            h_ref[section + 1, row] = jnp.where(inside(row), result, 0.0).astype(BF)

        slot = section * 3
        conv_loop(21 - 3 * section, h_ref.at[section], wf_ref.at[slot],
                  activate(p1_ref, a1_ref))
        conv_loop(20 - 3 * section, a1_ref.at[section], wf_ref.at[slot + 1],
                  activate(p2_ref, a2_ref))
        conv_loop(0 if section == DEPTH - 1 else 19 - 3 * section, a2_ref.at[section],
                  wf_ref.at[slot + 2], residual)
        return carry

    for section in range(DEPTH):
        slabs[section].wait()
        forward(section, 0)
    slabs[DEPTH].wait()

    def kernel_grad(layer, source, grads):
        wide_in, wide_out = [], []
        for row in range(OFF, OFF + OWN):
            wide_in.append(source[pl.ds(row - 1, 3)].reshape(3 * C, WID))
            out = grads[row].astype(F32)
            after = jnp.where(not_last[:C], pltpu.roll(out, WID - 1, 1), 0.0)
            before = jnp.where(not_first[:C], pltpu.roll(out, 1, 1), 0.0)
            wide_out.append(jnp.concatenate([after, out, before], axis=0).astype(BF))
        result = lax.dot_general(
            jnp.concatenate(wide_in, axis=1),
            jnp.concatenate(wide_out, axis=1),
            (((1,), (1,)), ((), ())),
            preferred_element_type=F32,
        )
        for kw in range(3):
            part = result[:, kw * C:(kw + 1) * C]
            packed = jnp.concatenate([part[:96], part[96:]], axis=1)
            wg_ref[pl.ds((layer * 3 + kw) * 96, 96), :] = packed.astype(BF)

    wg_ref[864:1024, :] = jnp.zeros((160, 128), BF)

    def backward(turn, carry):
        section = DEPTH - 1 - turn
        slot = section * 3

        def through(pre_ref, target):
            def finish(row, values):
                result = values * slope_of(pre_ref[section, row])
                target[section, row] = jnp.where(inside(row), result, 0.0).astype(BF)

            return finish

        def residual(row, values):
            result = g_ref[section + 1, row].astype(F32) + values
            g_ref[section, row] = jnp.where(inside(row), result, 0.0).astype(BF)

        conv_loop(2 + 3 * section, g_ref.at[section + 1], wb_ref.at[slot + 2], through(p2_ref, gp2_ref), section >= mine)
        conv_loop(1 + 3 * section, gp2_ref.at[section], wb_ref.at[slot + 1], through(p1_ref, gp1_ref), section >= mine)

        conv_loop(3 * section, gp1_ref.at[section], wb_ref.at[slot], residual, section >= mine)
        return carry

    for turn in range(DEPTH):
        backward(turn, 0)

    kernel_grad(2, a2_ref.at[mine], g_ref.at[mine + 1])
    kernel_grad(1, a1_ref.at[mine], gp2_ref.at[mine])
    kernel_grad(0, h_ref.at[mine], gp1_ref.at[mine])

    side = where_ref[3]
    kept = OFF + 4 * side
    sent = OFF + 4 * (1 - side)
    even_ref[0] = h_ref[mine + 1, pl.ds(kept, 4)]
    even_ref[1] = g_ref[mine, pl.ds(kept, 4)]
    odd_ref[0] = h_ref[mine + 1, pl.ds(sent, 4)]
    odd_ref[1] = g_ref[mine, pl.ds(sent, 4)]


def unpack_kernel(sum_ref, out_ref):
    for layer in range(3):
        for kw in range(3):
            base = (layer * 3 + kw) * 96
            block = sum_ref[base:base + 96, :].astype(F32)
            tall = jnp.concatenate([block[:, :C], block[:, C:]], axis=0)
            for kh in range(3):
                out_ref[0, layer, kh, kw] = tall[kh * C:(kh + 1) * C]


def vmem(count):
    return [pl.BlockSpec(memory_space=pltpu.VMEM)] * count


def sections_call(where, pieces, fwd, bwd):
    window = (WINDOW, C, WID)
    return pl.pallas_call(
        sections_kernel,
        out_shape=[
            jax.ShapeDtypeStruct((2, 4, C, WID), BF),
            jax.ShapeDtypeStruct((2, 4, C, WID), BF),
            jax.ShapeDtypeStruct((1024, 128), BF),
        ],
        in_specs=[pl.BlockSpec(memory_space=pltpu.SMEM)]
        + vmem(5)
        + [pl.BlockSpec(memory_space=pl.ANY)] * 2,
        out_specs=vmem(3),
        scratch_shapes=[
            pltpu.VMEM((DEPTH + 1,) + window, BF),
            pltpu.VMEM((DEPTH,) + window, BF),
            pltpu.VMEM((DEPTH,) + window, BF),
            pltpu.VMEM((DEPTH,) + window, F32),
            pltpu.VMEM((DEPTH,) + window, F32),
            pltpu.VMEM((DEPTH + 1,) + window, BF),
            pltpu.VMEM((DEPTH,) + window, BF),
            pltpu.VMEM((DEPTH,) + window, BF),
            pltpu.VMEM((12, 128, 768), BF),
            pltpu.VMEM((12, 128, 768), BF),
            pltpu.SemaphoreType.DMA((DEPTH + 1,)),
        ],
        compiler_params=pltpu.CompilerParams(vmem_limit_bytes=62 * 1024 * 1024),
        name="sections",
    )(where, *pieces, fwd, bwd)


SECTION = ("pair", "side")
BAND = ("z", "core")
CHIPS = 8


def on_device(images, weights, cotangent):
    pair, side = lax.axis_index("pair"), lax.axis_index("side")
    z, core = lax.axis_index("z"), lax.axis_index("core")
    section = 2 * pair + side
    where = jnp.stack([2 * pair + core, z * OWN, core, side, section]).astype(jnp.int32)

    raw = weights.reshape(27, 2, 32, C)
    raw = jnp.concatenate([raw[:, 0], raw[:, 1]], axis=-1).reshape(864, 128)
    near = lax.ppermute(
        raw,
        SECTION + ("core",),
        [
            (s * 2 + c, (s + 1 - 2 * c) % DEPTH * 2 + c)
            for s in range(DEPTH)
            for c in range(2)
        ],
    )
    half = lax.ppermute(
        jnp.where(core == 0, raw[:448], raw[416:]),
        SECTION,
        [(s, (s + 2) % DEPTH) for s in range(DEPTH)],
    )
    field = jnp.where(side == 0, jnp.stack([images[0], cotangent[0]]), jnp.stack([images[1], cotangent[1]]))
    center = field.transpose(0, 2, 1, 3).reshape(8, C, WID)
    swapped = [(i, i ^ 1) for i in range(2 * CHIPS)]

    def chips_away(value, chips):
        pairs = [
            (2 * z + c, 2 * (z + step) + c)
            for c, step in ((0, chips), (1, -chips))
            for z in range(CHIPS)
            if 0 <= z + step < CHIPS
        ]
        return lax.ppermute(value, BAND, pairs)

    upper = core == 0
    swap = lax.ppermute(center, BAND, swapped)
    first, last = jnp.where(upper, center, swap), jnp.where(upper, swap, center)
    chip = jnp.concatenate([first[0:4], last[0:4], first[4:8], last[4:8]])
    near_rows = chips_away(chip, 1)
    other_near = lax.ppermute(near_rows, BAND, swapped)
    far_rows = chips_away(
        jnp.where(
            upper,
            jnp.concatenate([near_rows[2:8], chip[0:8], chip[12:16]]),
            jnp.concatenate([chip[0:8], near_rows[0:6], chip[8:12]]),
        ),
        2,
    )
    near, where = lax.optimization_barrier((near, where))
    other_weights = lax.ppermute(jnp.concatenate([near, half]), BAND, swapped)
    fwd, bwd = pl.pallas_call(
        weight_blocks_kernel,
        out_shape=[jax.ShapeDtypeStruct((12, 128, 768), BF)] * 2,
        in_specs=[pl.BlockSpec(memory_space=pltpu.SMEM)] + vmem(4),
        out_specs=vmem(2),
        scratch_shapes=[pltpu.VMEM((864, 128), BF)],
        name="weight_blocks",
    )(where, raw, near, half, other_weights)
    far_rows, other_near, fwd, bwd = lax.optimization_barrier((far_rows, other_near, fwd, bwd))
    other_far = lax.ppermute(far_rows, BAND, swapped)

    even, odd, grads = sections_call(
        where,
        (chip, near_rows, far_rows, other_near, other_far),
        fwd,
        bwd,
    )

    parts = lax.all_to_all(grads.reshape(64, 16, 128), ("rep", "side", "z"), 0, 0, tiled=True)
    total = jnp.sum(parts.astype(F32), axis=0).astype(BF)
    turned = [(2 * q + c, 2 * c + q) for q in range(2) for c in range(2)]
    total = lax.ppermute(total, ("side", "core"), turned)
    summed = lax.all_to_all(
        jnp.broadcast_to(total[None], (64, 16, 128)), ("rep", "core", "z"), 0, 0, tiled=True
    ).reshape(1024, 128)

    even = lax.ppermute(even, ("side", "core"), turned)
    odd = lax.ppermute(
        odd, ("side", "core"), [(2 * q + c, 2 * c + 1 - q) for q in range(2) for c in range(2)]
    )
    zero = jnp.where(core == 0, even, odd)
    one = jnp.where(core == 0, odd, even)
    both = jnp.stack([zero, one]).transpose(1, 0, 3, 2, 4)

    weight_grads = pl.pallas_call(
        unpack_kernel,
        out_shape=jax.ShapeDtypeStruct((1, 3, 3, 3, C, C), F32),
        in_specs=vmem(1),
        out_specs=pl.BlockSpec(memory_space=pltpu.VMEM),
        name="unpack",
    )(summed)
    return both[0][None], both[1][None], weight_grads


def solution(mesh):
    finer = Mesh(
        mesh.devices.reshape(2, 2, CHIPS, 2, mesh.devices.shape[2]), SECTION + BAND + ("rep",)
    )
    in_specs = (
        P("rep", None, BAND, None),
        P(SECTION, None, None, None, None, None),
        P("rep", None, BAND, None),
    )
    out_specs = (
        P(SECTION, "rep", None, BAND, None),
        P(SECTION, "rep", None, BAND, None),
        P(SECTION, None, None, None, None, None),
    )
    return jax.shard_map(
        on_device, mesh=finer, in_specs=in_specs, out_specs=out_specs, check_vma=False
    )
```

```python
import jax
import jax.numpy as jnp
from jax import lax
from jax.experimental import pallas as pl
from jax.experimental.pallas import tpu as pltpu
from jax.sharding import Mesh
from jax.sharding import PartitionSpec as P

BF = jnp.bfloat16
F32 = jnp.float32
gelu_scale = 0.7978845608028654
cubic_coef = 0.044715

C = 64
WID = 128
ROWS = 64
OWN = 8
OFF = 24
WINDOW = 56
DEPTH = 4


def weight_blocks_kernel(where_ref, own, near, half, other, fwd_ref, bwd_ref, far):
    zero = jnp.zeros((C, C), BF)
    same = (
        lax.broadcasted_iota(jnp.int32, (C, C), 0) == lax.broadcasted_iota(jnp.int32, (C, C), 1)
    ).astype(F32).astype(BF)
    core = where_ref[2]
    far[pl.ds(pl.multiple_of(416 * core, 32), 448), :] = half[...]
    far[pl.ds(pl.multiple_of(416 * (1 - core), 32), 448), :] = other[864:1312, :]
    for piece, hop in ((own, 0), (near, 1 + 2 * core), (other, 3 - 2 * core), (far, 2)):
        section = lax.rem(where_ref[4] - hop + DEPTH, DEPTH)
        for layer in range(3):
            slot = section * 3 + layer
            for kw in range(3):
                taps = []
                for kh in range(3):
                    at = layer * 288 + (kh * 3 + kw) * 32
                    block = piece[at:at + 32, :]
                    taps.append(jnp.concatenate([block[:, :C], block[:, C:]], axis=0))
                tall = jnp.concatenate(taps + [zero] + [zero] + taps, axis=0)
                flat = lax.dot_general(
                    same, tall, (((1,), (1,)), ((), ())), preferred_element_type=F32
                ).astype(BF)
                here = slice(kw * 256, kw * 256 + 256)
                fwd_ref[slot, 0:C, here] = flat[:, 0:256]
                fwd_ref[slot, C:2 * C, here] = flat[:, 256:512]
                there = (2 - kw) * 256
                left = jnp.concatenate([taps[2], taps[1]], axis=1)
                middle = jnp.concatenate([taps[1], taps[0]], axis=1)
                bwd_ref[slot, 0:C, there:there + 128] = left
                bwd_ref[slot, 0:C, there + 128:there + 256] = jnp.concatenate([taps[0], zero], axis=1)
                bwd_ref[slot, C:2 * C, there:there + 128] = jnp.concatenate([zero, taps[2]], axis=1)
                bwd_ref[slot, C:2 * C, there + 128:there + 256] = middle


def sections_kernel(
    where_ref,
    chip_rows, near_rows, far_rows, other_near, other_far,
    wf_hbm, wb_hbm,
    even_ref, odd_ref, wg_ref,
    h_ref, a1_ref, a2_ref, p1_ref, p2_ref, g_ref, gp1_ref, gp2_ref, wf_ref, wb_ref, sems,
):
    mine = where_ref[0]
    first_row = where_ref[1]
    core = where_ref[2]
    slabs = [
        pltpu.make_async_copy(
            wf_hbm.at[3 * n:3 * n + 3], wf_ref.at[3 * n:3 * n + 3], sems.at[n]
        )
        for n in range(DEPTH)
    ] + [pltpu.make_async_copy(wb_hbm, wb_ref, sems.at[DEPTH])]
    for slab_copy in slabs:
        slab_copy.start()
    h_ref[0, 24:32] = chip_rows[0:8]
    g_ref[DEPTH, 24:32] = chip_rows[8:16]
    for one, two, lower in ((near_rows, far_rows, core), (other_near, other_far, 1 - core)):
        h_ref[0, pl.ds(16 + 16 * lower, 8)] = one[0:8]
        h_ref[0, pl.ds(2 + 38 * lower, 14)] = two[0:14]
        g_ref[DEPTH, pl.ds(16 + 16 * lower, 8)] = one[8:16]
        g_ref[DEPTH, pl.ds(12 + 28 * lower, 4)] = two[14:18]

    lane = lax.broadcasted_iota(jnp.int32, (128, WID), 1)
    not_first = lane > 0
    not_last = lane < WID - 1
    lane1 = lax.broadcasted_iota(jnp.int32, (1, WID), 1)
    keep_first = (lane1 > 0).astype(F32).astype(BF)
    keep_last = (lane1 < WID - 1).astype(F32).astype(BF)

    def inside(row):
        at = row - OFF + first_row
        return jnp.logical_and(at >= 0, at < ROWS)

    def conv_rows(row, count, source, slab, finish):
        rows = source[pl.ds(row - 1, count + 2)].reshape((count + 2) * C, WID)
        before = pltpu.roll(rows, 1, 1) * keep_first
        after = pltpu.roll(rows, WID - 1, 1) * keep_last
        products = []
        for at in range(0, count, 4):
            halves = []
            for part in (at, at + 2):
                cut = slice(part * C, (part + 4) * C)
                halves.append(jnp.concatenate([before[cut], rows[cut], after[cut]], axis=0))
            products.append(lax.dot_general(
                slab[...],
                jnp.concatenate(halves, axis=1),
                (((1,), (0,)), ((), ())),
                preferred_element_type=F32,
            ))
        for at, product in zip(range(0, count, 4), products):
            for half in range(2):
                for one in range(2):
                    finish(row + at + 2 * half + one, product[one * C:(one + 1) * C, half * WID:(half + 1) * WID])

    def conv_loop(reach, source, slab, finish, needed=None):
        start = OFF - reach
        count = -(-(8 + 2 * reach) // 4) * 4
        parts = -(-count // 28)
        size = -(-count // (4 * parts)) * 4
        for part in range(parts):
            @pl.when(mine >= 0 if needed is None else needed)
            def _(part=part):
                conv_rows(start + size * part, min(size, count - size * part), source, slab, finish)

    def tangent_of(values):
        return jnp.tanh(values * (gelu_scale + (gelu_scale * cubic_coef) * (values * values)))

    def slope_of(values):
        square = values * values
        tangent = jnp.tanh(values * (gelu_scale + (gelu_scale * cubic_coef) * square))
        return 0.5 * (1.0 + tangent) + (0.5 * values) * (1.0 - tangent * tangent) * (
            gelu_scale + (3.0 * gelu_scale * cubic_coef) * square
        )

    def forward(section, carry):
        def activate(pre_ref, act_ref):
            def finish(row, values):
                pre_ref[section, row] = values
                half = 0.5 * values
                act = half + half * tangent_of(values)
                act_ref[section, row] = jnp.where(inside(row), act, 0.0).astype(BF)

            return finish

        def residual(row, values):
            result = h_ref[section, row].astype(F32) + values
            h_ref[section + 1, row] = jnp.where(inside(row), result, 0.0).astype(BF)

        slot = section * 3
        conv_loop(21 - 3 * section, h_ref.at[section], wf_ref.at[slot],
                  activate(p1_ref, a1_ref))
        conv_loop(20 - 3 * section, a1_ref.at[section], wf_ref.at[slot + 1],
                  activate(p2_ref, a2_ref))
        conv_loop(0 if section == DEPTH - 1 else 19 - 3 * section, a2_ref.at[section],
                  wf_ref.at[slot + 2], residual)
        return carry

    for section in range(DEPTH):
        slabs[section].wait()
        forward(section, 0)
    slabs[DEPTH].wait()

    def kernel_grad(layer, source, grads):
        wide_in, wide_out = [], []
        for row in range(OFF, OFF + OWN):
            wide_in.append(source[pl.ds(row - 1, 3)].reshape(3 * C, WID))
            out = grads[row].astype(F32)
            after = jnp.where(not_last[:C], pltpu.roll(out, WID - 1, 1), 0.0)
            before = jnp.where(not_first[:C], pltpu.roll(out, 1, 1), 0.0)
            wide_out.append(jnp.concatenate([after, out, before], axis=0).astype(BF))
        result = lax.dot_general(
            jnp.concatenate(wide_in, axis=1),
            jnp.concatenate(wide_out, axis=1),
            (((1,), (1,)), ((), ())),
            preferred_element_type=F32,
        )
        for kw in range(3):
            part = result[:, kw * C:(kw + 1) * C]
            packed = jnp.concatenate([part[:96], part[96:]], axis=1)
            wg_ref[pl.ds((layer * 3 + kw) * 96, 96), :] = packed.astype(BF)

    wg_ref[864:1024, :] = jnp.zeros((160, 128), BF)

    def backward(turn, carry):
        section = DEPTH - 1 - turn
        slot = section * 3

        def through(pre_ref, target):
            def finish(row, values):
                result = values * slope_of(pre_ref[section, row])
                target[section, row] = jnp.where(inside(row), result, 0.0).astype(BF)

            return finish

        def residual(row, values):
            result = g_ref[section + 1, row].astype(F32) + values
            g_ref[section, row] = jnp.where(inside(row), result, 0.0).astype(BF)

        conv_loop(2 + 3 * section, g_ref.at[section + 1], wb_ref.at[slot + 2], through(p2_ref, gp2_ref), section >= mine)
        conv_loop(1 + 3 * section, gp2_ref.at[section], wb_ref.at[slot + 1], through(p1_ref, gp1_ref), section >= mine)

        conv_loop(3 * section, gp1_ref.at[section], wb_ref.at[slot], residual, section >= mine)
        return carry

    for turn in range(DEPTH):
        backward(turn, 0)

    kernel_grad(2, a2_ref.at[mine], g_ref.at[mine + 1])
    kernel_grad(1, a1_ref.at[mine], gp2_ref.at[mine])
    kernel_grad(0, h_ref.at[mine], gp1_ref.at[mine])

    side = where_ref[3]
    kept = OFF + 4 * side
    sent = OFF + 4 * (1 - side)
    even_ref[0] = h_ref[mine + 1, pl.ds(kept, 4)]
    even_ref[1] = g_ref[mine, pl.ds(kept, 4)]
    odd_ref[0] = h_ref[mine + 1, pl.ds(sent, 4)]
    odd_ref[1] = g_ref[mine, pl.ds(sent, 4)]


def unpack_kernel(sum_ref, out_ref):
    for layer in range(3):
        for kw in range(3):
            base = (layer * 3 + kw) * 96
            block = sum_ref[base:base + 96, :].astype(F32)
            tall = jnp.concatenate([block[:, :C], block[:, C:]], axis=0)
            for kh in range(3):
                out_ref[0, layer, kh, kw] = tall[kh * C:(kh + 1) * C]


def vmem(count):
    return [pl.BlockSpec(memory_space=pltpu.VMEM)] * count


def sections_call(where, pieces, fwd, bwd):
    window = (WINDOW, C, WID)
    return pl.pallas_call(
        sections_kernel,
        out_shape=[
            jax.ShapeDtypeStruct((2, 4, C, WID), BF),
            jax.ShapeDtypeStruct((2, 4, C, WID), BF),
            jax.ShapeDtypeStruct((1024, 128), BF),
        ],
        in_specs=[pl.BlockSpec(memory_space=pltpu.SMEM)]
        + vmem(5)
        + [pl.BlockSpec(memory_space=pl.ANY)] * 2,
        out_specs=vmem(3),
        scratch_shapes=[
            pltpu.VMEM((DEPTH + 1,) + window, BF),
            pltpu.VMEM((DEPTH,) + window, BF),
            pltpu.VMEM((DEPTH,) + window, BF),
            pltpu.VMEM((DEPTH,) + window, F32),
            pltpu.VMEM((DEPTH,) + window, F32),
            pltpu.VMEM((DEPTH + 1,) + window, BF),
            pltpu.VMEM((DEPTH,) + window, BF),
            pltpu.VMEM((DEPTH,) + window, BF),
            pltpu.VMEM((12, 128, 768), BF),
            pltpu.VMEM((12, 128, 768), BF),
            pltpu.SemaphoreType.DMA((DEPTH + 1,)),
        ],
        compiler_params=pltpu.CompilerParams(vmem_limit_bytes=62 * 1024 * 1024),
        name="sections",
    )(where, *pieces, fwd, bwd)


SECTION = ("pair", "side")
BAND = ("z", "core")
CHIPS = 8


def on_device(images, weights, cotangent):
    pair, side = lax.axis_index("pair"), lax.axis_index("side")
    z, core = lax.axis_index("z"), lax.axis_index("core")
    section = 2 * pair + side
    where = jnp.stack([2 * pair + core, z * OWN, core, side, section]).astype(jnp.int32)

    raw = weights.reshape(27, 2, 32, C)
    raw = jnp.concatenate([raw[:, 0], raw[:, 1]], axis=-1).reshape(864, 128)
    near = lax.ppermute(
        raw,
        SECTION + ("core",),
        [
            (s * 2 + c, (s + 1 - 2 * c) % DEPTH * 2 + c)
            for s in range(DEPTH)
            for c in range(2)
        ],
    )
    half = lax.ppermute(
        jnp.where(core == 0, raw[:448], raw[416:]),
        SECTION,
        [(s, (s + 2) % DEPTH) for s in range(DEPTH)],
    )
    field = jnp.where(side == 0, jnp.stack([images[0], cotangent[0]]), jnp.stack([images[1], cotangent[1]]))
    center = field.transpose(0, 2, 1, 3).reshape(8, C, WID)
    swapped = [(i, i ^ 1) for i in range(2 * CHIPS)]

    def chips_away(value, chips):
        pairs = [
            (2 * z + c, 2 * (z + step) + c)
            for c, step in ((0, chips), (1, -chips))
            for z in range(CHIPS)
            if 0 <= z + step < CHIPS
        ]
        return lax.ppermute(value, BAND, pairs)

    upper = core == 0
    swap = lax.ppermute(center, BAND, swapped)
    first, last = jnp.where(upper, center, swap), jnp.where(upper, swap, center)
    chip = jnp.concatenate([first[0:4], last[0:4], first[4:8], last[4:8]])
    near_rows = chips_away(chip, 1)
    other_near = lax.ppermute(near_rows, BAND, swapped)
    far_rows = chips_away(
        jnp.where(
            upper,
            jnp.concatenate([near_rows[2:8], chip[0:8], chip[12:16]]),
            jnp.concatenate([chip[0:8], near_rows[0:6], chip[8:12]]),
        ),
        2,
    )
    near, where = lax.optimization_barrier((near, where))
    other_weights = lax.ppermute(jnp.concatenate([near, half]), BAND, swapped)
    fwd, bwd = pl.pallas_call(
        weight_blocks_kernel,
        out_shape=[jax.ShapeDtypeStruct((12, 128, 768), BF)] * 2,
        in_specs=[pl.BlockSpec(memory_space=pltpu.SMEM)] + vmem(4),
        out_specs=vmem(2),
        scratch_shapes=[pltpu.VMEM((864, 128), BF)],
        name="weight_blocks",
    )(where, raw, near, half, other_weights)
    far_rows, other_near, fwd, bwd = lax.optimization_barrier((far_rows, other_near, fwd, bwd))
    other_far = lax.ppermute(far_rows, BAND, swapped)

    even, odd, grads = sections_call(
        where,
        (chip, near_rows, far_rows, other_near, other_far),
        fwd,
        bwd,
    )

    parts = lax.all_to_all(grads.reshape(64, 16, 128), ("rep", "z", "side"), 0, 0, tiled=True)
    total = jnp.sum(parts.astype(F32), axis=0).astype(BF)
    turned = [(2 * q + c, 2 * c + q) for q in range(2) for c in range(2)]
    total = lax.ppermute(total, ("side", "core"), turned)
    summed = lax.all_to_all(
        jnp.broadcast_to(total[None], (64, 16, 128)), ("rep", "z", "core"), 0, 0, tiled=True
    ).reshape(1024, 128)

    even = lax.ppermute(even, ("side", "core"), turned)
    odd = lax.ppermute(
        odd, ("side", "core"), [(2 * q + c, 2 * c + 1 - q) for q in range(2) for c in range(2)]
    )
    zero = jnp.where(core == 0, even, odd)
    one = jnp.where(core == 0, odd, even)
    both = jnp.stack([zero, one]).transpose(1, 0, 3, 2, 4)

    weight_grads = pl.pallas_call(
        unpack_kernel,
        out_shape=jax.ShapeDtypeStruct((1, 3, 3, 3, C, C), F32),
        in_specs=vmem(1),
        out_specs=pl.BlockSpec(memory_space=pltpu.VMEM),
        name="unpack",
    )(summed)
    return both[0][None], both[1][None], weight_grads


def solution(mesh):
    finer = Mesh(
        mesh.devices.reshape(2, 2, CHIPS, 2, mesh.devices.shape[2]), SECTION + BAND + ("rep",)
    )
    in_specs = (
        P("rep", None, BAND, None),
        P(SECTION, None, None, None, None, None),
        P("rep", None, BAND, None),
    )
    out_specs = (
        P(SECTION, "rep", None, BAND, None),
        P(SECTION, "rep", None, BAND, None),
        P(SECTION, None, None, None, None, None),
    )
    return jax.shard_map(
        on_device, mesh=finer, in_specs=in_specs, out_specs=out_specs, check_vma=False
    )
```

```python
import jax
import jax.numpy as jnp
from jax import lax
from jax.experimental import pallas as pl
from jax.experimental.pallas import tpu as pltpu
from jax.sharding import Mesh
from jax.sharding import PartitionSpec as P

BF = jnp.bfloat16
F32 = jnp.float32
gelu_scale = 0.7978845608028654
cubic_coef = 0.044715

C = 64
WID = 128
ROWS = 64
OWN = 8
OFF = 24
WINDOW = 56
DEPTH = 4


def weight_blocks_kernel(where_ref, own, near, half, other, fwd_ref, bwd_ref, far):
    zero = jnp.zeros((C, C), BF)
    same = (
        lax.broadcasted_iota(jnp.int32, (C, C), 0) == lax.broadcasted_iota(jnp.int32, (C, C), 1)
    ).astype(F32).astype(BF)
    core = where_ref[2]
    far[pl.ds(pl.multiple_of(416 * core, 32), 448), :] = half[...]
    far[pl.ds(pl.multiple_of(416 * (1 - core), 32), 448), :] = other[864:1312, :]
    for piece, hop in ((own, 0), (near, 1 + 2 * core), (other, 3 - 2 * core), (far, 2)):
        section = lax.rem(where_ref[4] - hop + DEPTH, DEPTH)
        for layer in range(3):
            slot = section * 3 + layer
            for kw in range(3):
                taps = []
                for kh in range(3):
                    at = layer * 288 + (kh * 3 + kw) * 32
                    block = piece[at:at + 32, :]
                    taps.append(jnp.concatenate([block[:, :C], block[:, C:]], axis=0))
                tall = jnp.concatenate(taps + [zero] + [zero] + taps, axis=0)
                flat = lax.dot_general(
                    same, tall, (((1,), (1,)), ((), ())), preferred_element_type=F32
                ).astype(BF)
                here = slice(kw * 256, kw * 256 + 256)
                fwd_ref[slot, 0:C, here] = flat[:, 0:256]
                fwd_ref[slot, C:2 * C, here] = flat[:, 256:512]
                there = (2 - kw) * 256
                left = jnp.concatenate([taps[2], taps[1]], axis=1)
                middle = jnp.concatenate([taps[1], taps[0]], axis=1)
                bwd_ref[slot, 0:C, there:there + 128] = left
                bwd_ref[slot, 0:C, there + 128:there + 256] = jnp.concatenate([taps[0], zero], axis=1)
                bwd_ref[slot, C:2 * C, there:there + 128] = jnp.concatenate([zero, taps[2]], axis=1)
                bwd_ref[slot, C:2 * C, there + 128:there + 256] = middle


def sections_kernel(
    where_ref,
    chip_rows, near_rows, far_rows, other_near, other_far,
    wf_hbm, wb_hbm,
    even_ref, odd_ref, wg_ref,
    h_ref, a1_ref, a2_ref, p1_ref, p2_ref, g_ref, gp1_ref, gp2_ref, wf_ref, wb_ref, sems,
):
    mine = where_ref[0]
    first_row = where_ref[1]
    core = where_ref[2]
    slabs = [
        pltpu.make_async_copy(
            wf_hbm.at[3 * n:3 * n + 3], wf_ref.at[3 * n:3 * n + 3], sems.at[n]
        )
        for n in range(DEPTH)
    ] + [pltpu.make_async_copy(wb_hbm, wb_ref, sems.at[DEPTH])]
    for slab_copy in slabs:
        slab_copy.start()
    h_ref[0, 24:32] = chip_rows[0:8]
    g_ref[DEPTH, 24:32] = chip_rows[8:16]
    for one, two, lower in ((near_rows, far_rows, core), (other_near, other_far, 1 - core)):
        h_ref[0, pl.ds(16 + 16 * lower, 8)] = one[0:8]
        h_ref[0, pl.ds(2 + 38 * lower, 14)] = two[0:14]
        g_ref[DEPTH, pl.ds(16 + 16 * lower, 8)] = one[8:16]
        g_ref[DEPTH, pl.ds(12 + 28 * lower, 4)] = two[14:18]

    lane = lax.broadcasted_iota(jnp.int32, (128, WID), 1)
    not_first = lane > 0
    not_last = lane < WID - 1
    lane1 = lax.broadcasted_iota(jnp.int32, (1, WID), 1)
    keep_first = (lane1 > 0).astype(F32).astype(BF)
    keep_last = (lane1 < WID - 1).astype(F32).astype(BF)

    def inside(row):
        at = row - OFF + first_row
        return jnp.logical_and(at >= 0, at < ROWS)

    def conv_rows(row, count, source, slab, finish):
        rows = source[pl.ds(row - 1, count + 2)].reshape((count + 2) * C, WID)
        before = pltpu.roll(rows, 1, 1) * keep_first
        after = pltpu.roll(rows, WID - 1, 1) * keep_last
        products = []
        for at in range(0, count, 4):
            halves = []
            for part in (at, at + 2):
                cut = slice(part * C, (part + 4) * C)
                halves.append(jnp.concatenate([before[cut], rows[cut], after[cut]], axis=0))
            products.append(lax.dot_general(
                slab[...],
                jnp.concatenate(halves, axis=1),
                (((1,), (0,)), ((), ())),
                preferred_element_type=F32,
            ))
        for at, product in zip(range(0, count, 4), products):
            for half in range(2):
                for one in range(2):
                    finish(row + at + 2 * half + one, product[one * C:(one + 1) * C, half * WID:(half + 1) * WID])

    def conv_loop(reach, source, slab, finish, needed=None):
        start = OFF - reach
        count = -(-(8 + 2 * reach) // 4) * 4
        parts = -(-count // 28)
        size = -(-count // (4 * parts)) * 4
        for part in range(parts):
            @pl.when(mine >= 0 if needed is None else needed)
            def _(part=part):
                conv_rows(start + size * part, min(size, count - size * part), source, slab, finish)

    def tangent_of(values):
        return jnp.tanh(values * (gelu_scale + (gelu_scale * cubic_coef) * (values * values)))

    def slope_of(values):
        square = values * values
        tangent = jnp.tanh(values * (gelu_scale + (gelu_scale * cubic_coef) * square))
        return 0.5 * (1.0 + tangent) + (0.5 * values) * (1.0 - tangent * tangent) * (
            gelu_scale + (3.0 * gelu_scale * cubic_coef) * square
        )

    def forward(section, carry):
        def activate(pre_ref, act_ref):
            def finish(row, values):
                pre_ref[section, row] = values
                half = 0.5 * values
                act = half + half * tangent_of(values)
                act_ref[section, row] = jnp.where(inside(row), act, 0.0).astype(BF)

            return finish

        def residual(row, values):
            result = h_ref[section, row].astype(F32) + values
            h_ref[section + 1, row] = jnp.where(inside(row), result, 0.0).astype(BF)

        slot = section * 3
        conv_loop(21 - 3 * section, h_ref.at[section], wf_ref.at[slot],
                  activate(p1_ref, a1_ref))
        conv_loop(20 - 3 * section, a1_ref.at[section], wf_ref.at[slot + 1],
                  activate(p2_ref, a2_ref))
        conv_loop(0 if section == DEPTH - 1 else 19 - 3 * section, a2_ref.at[section],
                  wf_ref.at[slot + 2], residual)
        return carry

    for section in range(DEPTH):
        slabs[section].wait()
        forward(section, 0)
    slabs[DEPTH].wait()

    def kernel_grad(layer, source, grads):
        wide_in, wide_out = [], []
        for row in range(OFF, OFF + OWN):
            wide_in.append(source[pl.ds(row - 1, 3)].reshape(3 * C, WID))
            out = grads[row].astype(F32)
            after = jnp.where(not_last[:C], pltpu.roll(out, WID - 1, 1), 0.0)
            before = jnp.where(not_first[:C], pltpu.roll(out, 1, 1), 0.0)
            wide_out.append(jnp.concatenate([after, out, before], axis=0).astype(BF))
        result = lax.dot_general(
            jnp.concatenate(wide_in, axis=1),
            jnp.concatenate(wide_out, axis=1),
            (((1,), (1,)), ((), ())),
            preferred_element_type=F32,
        )
        for kw in range(3):
            part = result[:, kw * C:(kw + 1) * C]
            packed = jnp.concatenate([part[:96], part[96:]], axis=1)
            wg_ref[pl.ds((layer * 3 + kw) * 96, 96), :] = packed.astype(BF)

    wg_ref[864:1024, :] = jnp.zeros((160, 128), BF)

    def backward(turn, carry):
        section = DEPTH - 1 - turn
        slot = section * 3

        def through(pre_ref, target):
            def finish(row, values):
                result = values * slope_of(pre_ref[section, row])
                target[section, row] = jnp.where(inside(row), result, 0.0).astype(BF)

            return finish

        def residual(row, values):
            result = g_ref[section + 1, row].astype(F32) + values
            g_ref[section, row] = jnp.where(inside(row), result, 0.0).astype(BF)

        conv_loop(2 + 3 * section, g_ref.at[section + 1], wb_ref.at[slot + 2], through(p2_ref, gp2_ref), section >= mine)
        conv_loop(1 + 3 * section, gp2_ref.at[section], wb_ref.at[slot + 1], through(p1_ref, gp1_ref), section >= mine)

        conv_loop(3 * section, gp1_ref.at[section], wb_ref.at[slot], residual, section >= mine)
        return carry

    for turn in range(DEPTH):
        backward(turn, 0)

    kernel_grad(2, a2_ref.at[mine], g_ref.at[mine + 1])
    kernel_grad(1, a1_ref.at[mine], gp2_ref.at[mine])
    kernel_grad(0, h_ref.at[mine], gp1_ref.at[mine])

    side = where_ref[3]
    kept = OFF + 4 * side
    sent = OFF + 4 * (1 - side)
    even_ref[0] = h_ref[mine + 1, pl.ds(kept, 4)]
    even_ref[1] = g_ref[mine, pl.ds(kept, 4)]
    odd_ref[0] = h_ref[mine + 1, pl.ds(sent, 4)]
    odd_ref[1] = g_ref[mine, pl.ds(sent, 4)]


def unpack_kernel(sum_ref, out_ref):
    for layer in range(3):
        for kw in range(3):
            base = (layer * 3 + kw) * 96
            block = sum_ref[base:base + 96, :].astype(F32)
            tall = jnp.concatenate([block[:, :C], block[:, C:]], axis=0)
            for kh in range(3):
                out_ref[0, layer, kh, kw] = tall[kh * C:(kh + 1) * C]


def vmem(count):
    return [pl.BlockSpec(memory_space=pltpu.VMEM)] * count


def sections_call(where, pieces, fwd, bwd):
    window = (WINDOW, C, WID)
    return pl.pallas_call(
        sections_kernel,
        out_shape=[
            jax.ShapeDtypeStruct((2, 4, C, WID), BF),
            jax.ShapeDtypeStruct((2, 4, C, WID), BF),
            jax.ShapeDtypeStruct((1024, 128), BF),
        ],
        in_specs=[pl.BlockSpec(memory_space=pltpu.SMEM)]
        + vmem(5)
        + [pl.BlockSpec(memory_space=pl.ANY)] * 2,
        out_specs=vmem(3),
        scratch_shapes=[
            pltpu.VMEM((DEPTH + 1,) + window, BF),
            pltpu.VMEM((DEPTH,) + window, BF),
            pltpu.VMEM((DEPTH,) + window, BF),
            pltpu.VMEM((DEPTH,) + window, F32),
            pltpu.VMEM((DEPTH,) + window, F32),
            pltpu.VMEM((DEPTH + 1,) + window, BF),
            pltpu.VMEM((DEPTH,) + window, BF),
            pltpu.VMEM((DEPTH,) + window, BF),
            pltpu.VMEM((12, 128, 768), BF),
            pltpu.VMEM((12, 128, 768), BF),
            pltpu.SemaphoreType.DMA((DEPTH + 1,)),
        ],
        compiler_params=pltpu.CompilerParams(vmem_limit_bytes=62 * 1024 * 1024),
        name="sections",
    )(where, *pieces, fwd, bwd)


SECTION = ("pair", "side")
BAND = ("z", "core")
CHIPS = 8


def on_device(images, weights, cotangent):
    pair, side = lax.axis_index("pair"), lax.axis_index("side")
    z, core = lax.axis_index("z"), lax.axis_index("core")
    section = 2 * pair + side
    where = jnp.stack([2 * pair + core, z * OWN, core, side, section]).astype(jnp.int32)

    raw = weights.reshape(27, 2, 32, C)
    raw = jnp.concatenate([raw[:, 0], raw[:, 1]], axis=-1).reshape(864, 128)
    near = lax.ppermute(
        raw,
        SECTION + ("core",),
        [
            (s * 2 + c, (s + 1 - 2 * c) % DEPTH * 2 + c)
            for s in range(DEPTH)
            for c in range(2)
        ],
    )
    half = lax.ppermute(
        jnp.where(core == 0, raw[:448], raw[416:]),
        SECTION,
        [(s, (s + 2) % DEPTH) for s in range(DEPTH)],
    )
    field = jnp.where(side == 0, jnp.stack([images[0], cotangent[0]]), jnp.stack([images[1], cotangent[1]]))
    center = field.transpose(0, 2, 1, 3).reshape(8, C, WID)
    swapped = [(i, i ^ 1) for i in range(2 * CHIPS)]

    def chips_away(value, chips):
        pairs = [
            (2 * z + c, 2 * (z + step) + c)
            for c, step in ((0, chips), (1, -chips))
            for z in range(CHIPS)
            if 0 <= z + step < CHIPS
        ]
        return lax.ppermute(value, BAND, pairs)

    upper = core == 0
    swap = lax.ppermute(center, BAND, swapped)
    first, last = jnp.where(upper, center, swap), jnp.where(upper, swap, center)
    chip = jnp.concatenate([first[0:4], last[0:4], first[4:8], last[4:8]])
    near_rows = chips_away(chip, 1)
    other_near = lax.ppermute(near_rows, BAND, swapped)
    far_rows = chips_away(
        jnp.where(
            upper,
            jnp.concatenate([near_rows[2:8], chip[0:8], chip[12:16]]),
            jnp.concatenate([chip[0:8], near_rows[0:6], chip[8:12]]),
        ),
        2,
    )
    near, where = lax.optimization_barrier((near, where))
    other_weights = lax.ppermute(jnp.concatenate([near, half]), BAND, swapped)
    fwd, bwd = pl.pallas_call(
        weight_blocks_kernel,
        out_shape=[jax.ShapeDtypeStruct((12, 128, 768), BF)] * 2,
        in_specs=[pl.BlockSpec(memory_space=pltpu.SMEM)] + vmem(4),
        out_specs=vmem(2),
        scratch_shapes=[pltpu.VMEM((864, 128), BF)],
        name="weight_blocks",
    )(where, raw, near, half, other_weights)
    far_rows, other_near, fwd, bwd = lax.optimization_barrier((far_rows, other_near, fwd, bwd))
    other_far = lax.ppermute(far_rows, BAND, swapped)

    even, odd, grads = sections_call(
        where,
        (chip, near_rows, far_rows, other_near, other_far),
        fwd,
        bwd,
    )

    parts = lax.all_to_all(grads.reshape(64, 16, 128), ("z", "rep", "side"), 0, 0, tiled=True)
    total = jnp.sum(parts.astype(F32), axis=0).astype(BF)
    turned = [(2 * q + c, 2 * c + q) for q in range(2) for c in range(2)]
    total = lax.ppermute(total, ("side", "core"), turned)
    summed = lax.all_to_all(
        jnp.broadcast_to(total[None], (64, 16, 128)), ("z", "rep", "core"), 0, 0, tiled=True
    ).reshape(1024, 128)

    even = lax.ppermute(even, ("side", "core"), turned)
    odd = lax.ppermute(
        odd, ("side", "core"), [(2 * q + c, 2 * c + 1 - q) for q in range(2) for c in range(2)]
    )
    zero = jnp.where(core == 0, even, odd)
    one = jnp.where(core == 0, odd, even)
    both = jnp.stack([zero, one]).transpose(1, 0, 3, 2, 4)

    weight_grads = pl.pallas_call(
        unpack_kernel,
        out_shape=jax.ShapeDtypeStruct((1, 3, 3, 3, C, C), F32),
        in_specs=vmem(1),
        out_specs=pl.BlockSpec(memory_space=pltpu.VMEM),
        name="unpack",
    )(summed)
    return both[0][None], both[1][None], weight_grads


def solution(mesh):
    finer = Mesh(
        mesh.devices.reshape(2, 2, CHIPS, 2, mesh.devices.shape[2]), SECTION + BAND + ("rep",)
    )
    in_specs = (
        P("rep", None, BAND, None),
        P(SECTION, None, None, None, None, None),
        P("rep", None, BAND, None),
    )
    out_specs = (
        P(SECTION, "rep", None, BAND, None),
        P(SECTION, "rep", None, BAND, None),
        P(SECTION, None, None, None, None, None),
    )
    return jax.shard_map(
        on_device, mesh=finer, in_specs=in_specs, out_specs=out_specs, check_vma=False
    )
```
